512 devices in a mesh: dom: 128 (over y, z, core), grp: 4 (over x).
Axes of the slice: x: 4, y: 8, z: 8, core: 2. Of those that a mesh axis runs over, the one named last changes fastest.
Arguments:
- node_latent: bfloat16 [65536, 512], P(('dom', 'grp')), may hold values from -6 to 6
- edge_latent: bfloat16 [262144, 512], P(('dom', 'grp')), may hold values from -6 to 6
- coarse_edge_latent: bfloat16 [16384, 512], P('dom'), may hold values from -6 to 6
- w_source: bfloat16 [512, 512], replicated, may hold values from -0.25 to 0.25
- w_target: bfloat16 [512, 512], replicated, may hold values from -0.25 to 0.25
- w_node: bfloat16 [512, 512], replicated, may hold values from -0.25 to 0.25
- cotangent: bfloat16 [65536, 512], P(('dom', 'grp')), may hold values from -6 to 6
- halo_rows: int32 [512, 2, 32], P(('dom', 'grp')), may hold values from -1 to 127, as said below
- fine_src: int32 [262144], P(('dom', 'grp')), may hold values from -1 to 191, as said below
- fine_dst: int32 [262144], P(('dom', 'grp')), may hold values from -1 to 127, as said below
- coarse_src: int32 [16384], P('dom'), may hold values from -1 to 31, as said below
- coarse_dst: int32 [16384], P('dom'), may hold values from -1 to 31, as said below
- intersection_ids: int32 [2, 65536], P(None, ('dom', 'grp')), may hold values from 0 to 31, as said below
- intersection_weights: float32 [2, 65536], P(None, ('dom', 'grp')), may hold values from 0.05 to 0.5
Outputs:
- updated: bfloat16 [65536, 512], P(('dom', 'grp'))
- grad_latent: bfloat16 [65536, 512], P(('dom', 'grp'))
- grad_source: float32 [262144], P(('dom', 'grp'))
- grad_target: float32 [262144], P(('dom', 'grp'))
- grad_node: float32 [262144], P(('dom', 'grp'))
The draws below stay inside these ranges and needn't reach their ends.
Inputs may be any that keep to these rules, and one draw needn't show every extreme that they name: `halo_rows`: in each list the first entries are rows of the subdomain, the rest -1; subdomain 0 sends nothing to side 0 and the last subdomain nothing to side 1. Per subdomain, the used edge slots come first and the others are -1, in fine_src and fine_dst alike; between 256 and 512 are used, some subdomain uses all. A source below 128 is a local row, 128 + j the j-th filled side-1 entry of the subdomain below, 160 + j the j-th filled side-0 entry of the subdomain above. `fine_dst`: -1 exactly where fine_src is -1. `coarse_src`: per group, the used slots come first, the others are -1 in both coarse lists; between 64 and 128 are used. `coarse_dst`: -1 exactly where coarse_src is -1. `intersection_ids`: coarse nodes of the fine node's own group; coarse node c is owned by the group's member c // 8.
All inputs are finite; a program needn't handle non-finite values.
Results may differ from the reference program's by a relative error of at most 0.017.
Values may be sent and summed in bfloat16 or wider, within the bound.
A program may use at most 64 MiB of HBM per device.

```python
import math
import jax
import jax.numpy as jnp
from jax import lax

LATENT = 512
NODES_DEV = 128
INTERSECTIONS = 2
EDGES_DEV = 512
SEND_MOST = 32
COARSE_DEV = 8
COARSE_GROUP = 32
COARSE_EDGES = 128
SUBDOMAINS = 512
GROUPS = 128
FINE_NODES = 65536
FINE_EDGES = 262144
COARSE_EDGES_ALL = 16384
N_DOM = 128
N_GRP = 4


def halo_counts(key):
    key = jax.random.fold_in(key, 501)
    counts = SEND_MOST - jax.random.randint(key, (SUBDOMAINS, 2), 0, SEND_MOST // 2 + 1)
    counts = counts.at[1, :].set(SEND_MOST).at[0, 1].set(SEND_MOST).at[2, 0].set(SEND_MOST)
    counts = counts.at[0, 0].set(0).at[SUBDOMAINS - 1, 1].set(0)
    return counts


def edge_totals(key):
    key = jax.random.fold_in(key, 502)
    totals = EDGES_DEV // 2 + jax.random.randint(key, (SUBDOMAINS,), 0, EDGES_DEV // 2 + 1)
    return totals.at[SUBDOMAINS // 2].set(EDGES_DEV).at[0].set(EDGES_DEV // 2)


def coarse_totals(key):
    key = jax.random.fold_in(key, 503)
    totals = COARSE_EDGES // 2 + jax.random.randint(key, (GROUPS,), 0, COARSE_EDGES // 2 + 1)
    return totals.at[0].set(COARSE_EDGES).at[GROUPS - 1].set(COARSE_EDGES // 2)


def draw_halo_rows(key, part):
    counts = halo_counts(key)
    key = jax.random.fold_in(key, 11)
    picked = jax.random.randint(key, (SUBDOMAINS, 2, SEND_MOST), 0, NODES_DEV)
    slot_index = lax.broadcasted_iota(jnp.int32, (SUBDOMAINS, 2, SEND_MOST), 2)
    picked = jnp.where(slot_index < counts[:, :, None], picked, -1)
    return picked.at[1, 0, 0].set(NODES_DEV - 1)


def draw_fine_src(key, part):
    counts = halo_counts(key)
    totals = edge_totals(key)
    key = jax.random.fold_in(key, 12)
    subkeys = jax.random.split(key, 4)
    shape = (SUBDOMAINS, EDGES_DEV)
    local_pick = jax.random.randint(subkeys[0], shape, 0, NODES_DEV)
    which_side = jax.random.randint(subkeys[1], shape, 0, 2)
    choose = jax.random.randint(subkeys[2], shape, 0, 4)
    raw_bits = jax.random.randint(subkeys[3], shape, 0, 1 << 20)
    nothing = jnp.zeros((1,), jnp.int32)
    from_lower = jnp.concatenate([nothing, counts[:-1, 1]])
    from_upper = jnp.concatenate([counts[1:, 0], nothing])
    available = jnp.where(which_side == 0, from_lower[:, None], from_upper[:, None])
    slot_index = raw_bits % jnp.maximum(available, 1)
    remote = NODES_DEV + which_side * SEND_MOST + slot_index
    sources = jnp.where((choose == 0) & (available > 0), remote, local_pick)
    position = lax.broadcasted_iota(jnp.int32, shape, 1)
    sources = jnp.where(position < totals[:, None], sources, -1)
    sources = sources.at[1, 0].set(NODES_DEV + 2 * SEND_MOST - 1).at[1, 1].set(NODES_DEV + SEND_MOST - 1)
    return sources.reshape(FINE_EDGES)


def draw_fine_dst(key, part):
    totals = edge_totals(key)
    key = jax.random.fold_in(key, 13)
    shape = (SUBDOMAINS, EDGES_DEV)
    targets = jax.random.randint(key, shape, 0, NODES_DEV)
    position = lax.broadcasted_iota(jnp.int32, shape, 1)
    targets = jnp.where(position < totals[:, None], targets, -1)
    return targets.at[1, 2].set(NODES_DEV - 1).reshape(FINE_EDGES)


def draw_coarse_src(key, part):
    totals = coarse_totals(key)
    key = jax.random.fold_in(key, 14)
    shape = (GROUPS, COARSE_EDGES)
    sources = jax.random.randint(key, shape, 0, COARSE_GROUP)
    position = lax.broadcasted_iota(jnp.int32, shape, 1)
    sources = jnp.where(position < totals[:, None], sources, -1)
    return sources.at[0, 0].set(COARSE_GROUP - 1).reshape(COARSE_EDGES_ALL)


def draw_coarse_dst(key, part):
    totals = coarse_totals(key)
    key = jax.random.fold_in(key, 15)
    shape = (GROUPS, COARSE_EDGES)
    targets = jax.random.randint(key, shape, 0, COARSE_GROUP)
    position = lax.broadcasted_iota(jnp.int32, shape, 1)
    targets = jnp.where(position < totals[:, None], targets, -1)
    return targets.at[0, 0].set(COARSE_GROUP - 1).reshape(COARSE_EDGES_ALL)


def draw_intersection_ids(key, part):
    key = jax.random.fold_in(key, 16)
    subkeys = jax.random.split(key, 2)
    device = lax.broadcasted_iota(jnp.int32, (FINE_NODES,), 0) // NODES_DEV
    member = device % (COARSE_GROUP // COARSE_DEV)
    primary = member * COARSE_DEV + jax.random.randint(subkeys[0], (FINE_NODES,), 0, COARSE_DEV)
    second = jax.random.randint(subkeys[1], (FINE_NODES,), 0, COARSE_GROUP)
    stacked = jnp.stack([primary, second], axis=0)
    return stacked.at[1, 0].set(0).at[1, 1].set(COARSE_GROUP - 1)


def block_levels(key, shape, shards, smallest, high):
    def one(dim, parts):
        draws = jax.random.uniform(jax.random.fold_in(jax.random.fold_in(key, 6), dim), (parts,), jnp.float32, smallest / len(shards), high / len(shards))
        return jnp.repeat(jnp.exp(draws), shape[dim] // parts).reshape((-1,) + (1,) * (len(shape) - dim - 1))

    factor_of = one(*shards[0])
    for cut in shards[1:]:
        factor_of = factor_of * one(*cut)
    return factor_of


def normal_values(stream_key, shape, deviation, most, cuts=(), kind=jnp.bfloat16):
    values = deviation * jax.random.normal(stream_key, shape, jnp.float32)
    if cuts:
        values = values * block_levels(stream_key, shape, cuts, -0.22, 0.18)
    return jnp.clip(values, -most, most).astype(kind)


def setup_inputs(seed: int = 0) -> dict:
    key_list = jax.random.split(jax.random.key(seed), 15)
    return {
        "node_latent": normal_values(key_list[0], (FINE_NODES, LATENT), 1.0, 6.0, ((0, 512),)),
        "edge_latent": normal_values(key_list[1], (FINE_EDGES, LATENT), 1.0, 6.0, ((0, 512),)),
        "coarse_edge_latent": normal_values(key_list[2], (COARSE_EDGES_ALL, LATENT), 1.0, 6.0, ((0, 128),)),
        "w_source": normal_values(key_list[3], (LATENT, LATENT), LATENT ** -0.5, 0.25),
        "w_target": normal_values(key_list[4], (LATENT, LATENT), LATENT ** -0.5, 0.25),
        "w_node": normal_values(key_list[5], (LATENT, LATENT), LATENT ** -0.5, 0.25),
        "cotangent": normal_values(key_list[6], (FINE_NODES, LATENT), 1.0, 6.0, ((0, 512),)),
        "halo_rows": draw_halo_rows(jax.random.fold_in(key_list[14], 71), 0),
        "fine_src": draw_fine_src(jax.random.fold_in(key_list[14], 71), 0),
        "fine_dst": draw_fine_dst(jax.random.fold_in(key_list[14], 71), 0),
        "coarse_src": draw_coarse_src(jax.random.fold_in(key_list[14], 71), 0),
        "coarse_dst": draw_coarse_dst(jax.random.fold_in(key_list[14], 71), 0),
        "intersection_ids": draw_intersection_ids(jax.random.fold_in(key_list[14], 71), 0),
        "intersection_weights": jnp.clip(jnp.exp(math.log(0.5) - 2.3025851 * jax.random.uniform(key_list[13], (INTERSECTIONS, FINE_NODES), jnp.float32) ** block_levels(key_list[13], (INTERSECTIONS, FINE_NODES), ((1, 512),), -0.2, 0.2)), 0.05, 0.5),
    }


EPSILON = 1e-06

def select_rows(values, positions):
    present = (positions >= 0).astype(values.dtype)
    return jnp.take(values, jnp.maximum(positions, 0), axis=0) * present[:, None]

def gather_sum(values, positions, extent):
    target_slot = jnp.where(positions >= 0, positions, extent)
    return jax.ops.segment_sum(values, target_slot, num_segments=extent + 1)[:extent]

def silu_slope(preact):
    logistic = jax.nn.sigmoid(preact)
    return logistic * (1.0 + preact * (1.0 - logistic))

def layer_forward(node_table, local_rows, edge_rows, sources, targets, w_source, w_target, w_node):
    proj_source = jnp.dot(node_table, w_source, preferred_element_type=jnp.float32)
    proj_target = jnp.dot(local_rows, w_target, preferred_element_type=jnp.float32)
    preact = edge_rows.astype(jnp.float32) + select_rows(proj_source, sources) + select_rows(proj_target, targets)
    message = jax.nn.silu(preact).astype(jnp.bfloat16)
    summed = gather_sum(message.astype(jnp.float32), targets, local_rows.shape[0])
    inverse_rms = lax.rsqrt(lax.optimization_barrier(jnp.mean(summed * summed, axis=-1, keepdims=True)) + EPSILON)
    normed = summed * inverse_rms
    normed_half = normed.astype(jnp.bfloat16)
    result = local_rows.astype(jnp.float32) + jnp.dot(normed_half, w_node, preferred_element_type=jnp.float32)
    return (result, (preact, normed, inverse_rms, normed_half))

def layer_backward(grad_out, saved, node_table, local_rows, sources, targets, w_source, w_target, w_node):
    preact, normed, inverse_rms, normed_half = saved
    grad_half = grad_out.astype(jnp.bfloat16)
    term_node = jnp.dot(normed_half.T, grad_half, preferred_element_type=jnp.float32)
    grad_normed = jnp.dot(grad_half, w_node.T, preferred_element_type=jnp.float32)
    grad_summed = inverse_rms * (grad_normed - normed * lax.optimization_barrier(jnp.mean(grad_normed * normed, axis=-1, keepdims=True)))
    grad_preact = (select_rows(grad_summed, targets) * silu_slope(preact)).astype(jnp.bfloat16)
    grad_wide = grad_preact.astype(jnp.float32)
    grad_src = gather_sum(grad_wide, sources, node_table.shape[0]).astype(jnp.bfloat16)
    grad_dst = gather_sum(grad_wide, targets, local_rows.shape[0]).astype(jnp.bfloat16)
    term_source = jnp.dot(node_table.T, grad_src, preferred_element_type=jnp.float32)
    term_target = jnp.dot(local_rows.T, grad_dst, preferred_element_type=jnp.float32)
    grad_table = jnp.dot(grad_src, w_source.T, preferred_element_type=jnp.float32)
    grad_local = grad_out + jnp.dot(grad_dst, w_target.T, preferred_element_type=jnp.float32)
    return (grad_table, grad_local, (term_source, term_target, term_node))

def reference(node_latent, edge_latent, coarse_edge_latent, w_source, w_target, w_node, cotangent, halo_rows, fine_src, fine_dst, coarse_src, coarse_dst, intersection_ids, intersection_weights):
    domains = N_DOM * N_GRP
    node_blocks = node_latent.reshape(domains, NODES_DEV, LATENT)
    edge_blocks = edge_latent.reshape(domains, EDGES_DEV, LATENT)
    source_blocks = fine_src.reshape(domains, EDGES_DEV)
    target_blocks = fine_dst.reshape(domains, EDGES_DEV)
    send_lists = halo_rows.reshape(domains, 2 * SEND_MOST)
    send_block = jax.vmap(select_rows)(node_blocks, send_lists)
    empty_rows = jnp.zeros((1, SEND_MOST, LATENT), jnp.bfloat16)
    from_lower = jnp.concatenate([empty_rows, send_block[:-1, SEND_MOST:]], axis=0)
    from_upper = jnp.concatenate([send_block[1:, :SEND_MOST], empty_rows], axis=0)
    tables = jnp.concatenate([node_blocks, from_lower, from_upper], axis=1)

    def fine_forward(inputs_now):
        node_table, local_rows, edge_rows, sources, targets = inputs_now
        return layer_forward(node_table, local_rows, edge_rows, sources, targets, w_source, w_target, w_node)[0]
    fine_out = lax.map(fine_forward, (tables, node_blocks, edge_blocks, source_blocks, target_blocks))
    group_rows = N_GRP * NODES_DEV
    coarse_count = COARSE_DEV * N_GRP
    group_ids = intersection_ids.reshape(INTERSECTIONS, N_DOM, group_rows).transpose(1, 0, 2)
    group_weights = intersection_weights.reshape(INTERSECTIONS, N_DOM, group_rows).transpose(1, 0, 2)

    def restrict(values, ids_now, weights_now):
        running = jnp.zeros((coarse_count, LATENT), jnp.float32)
        for intersection in range(INTERSECTIONS):
            running = running + gather_sum(weights_now[intersection][:, None] * values, ids_now[intersection], coarse_count)
        return running

    def prolong(values, ids_now, weights_now):
        running = jnp.zeros((group_rows, LATENT), jnp.float32)
        for intersection in range(INTERSECTIONS):
            running = running + weights_now[intersection][:, None] * select_rows(values, ids_now[intersection])
        return running
    fine_grouped = fine_out.reshape(N_DOM, group_rows, LATENT)
    coarse_in = jax.vmap(restrict)(fine_grouped, group_ids, group_weights)
    coarse_half = coarse_in.astype(jnp.bfloat16)
    coarse_edges = coarse_edge_latent.reshape(N_DOM, COARSE_EDGES, LATENT)
    coarse_sources = coarse_src.reshape(N_DOM, COARSE_EDGES)
    coarse_targets = coarse_dst.reshape(N_DOM, COARSE_EDGES)

    def coarse_forward(inputs_now):
        half_rows, edge_rows, sources, targets = inputs_now
        return layer_forward(half_rows, half_rows, edge_rows, sources, targets, w_source, w_target, w_node)[0]
    coarse_out = lax.map(coarse_forward, (coarse_half, coarse_edges, coarse_sources, coarse_targets))
    updated = fine_grouped + jax.vmap(prolong)(coarse_out, group_ids, group_weights)
    updated = updated.reshape(FINE_NODES, LATENT).astype(jnp.bfloat16)
    grad_rows = cotangent.reshape(N_DOM, group_rows, LATENT).astype(jnp.float32)
    grad_coarse = jax.vmap(restrict)(grad_rows, group_ids, group_weights)

    def coarse_backward(totals, inputs_now):
        half_rows, edge_rows, sources, targets, grad_out = inputs_now
        saved = layer_forward(half_rows, half_rows, edge_rows, sources, targets, w_source, w_target, w_node)[1]
        grad_table, grad_local, terms = layer_backward(grad_out, saved, half_rows, half_rows, sources, targets, w_source, w_target, w_node)
        totals = tuple((before + term for before, term in zip(totals, terms)))
        return (totals, grad_table + grad_local)
    initial = tuple((jnp.zeros((LATENT, LATENT), jnp.float32) for _ in range(3)))
    coarse_terms, grad_coarse_in = lax.scan(coarse_backward, initial, (coarse_half, coarse_edges, coarse_sources, coarse_targets, grad_coarse))
    grad_fine = grad_rows + jax.vmap(prolong)(grad_coarse_in, group_ids, group_weights)
    grad_fine = grad_fine.reshape(domains, NODES_DEV, LATENT)

    def fine_backward(totals, inputs_now):
        node_table, local_rows, edge_rows, sources, targets, grad_out = inputs_now
        saved = layer_forward(node_table, local_rows, edge_rows, sources, targets, w_source, w_target, w_node)[1]
        grad_table, grad_local, terms = layer_backward(grad_out, saved, node_table, local_rows, sources, targets, w_source, w_target, w_node)
        totals = tuple((before + term for before, term in zip(totals, terms)))
        return (totals, (grad_local + grad_table[:NODES_DEV], grad_table[NODES_DEV:]))
    totals, (grad_own, grad_halo) = lax.scan(fine_backward, coarse_terms, (tables, node_blocks, edge_blocks, source_blocks, target_blocks, grad_fine))
    empty_grad = jnp.zeros((1, SEND_MOST, LATENT), jnp.float32)
    back_lower = jnp.concatenate([empty_grad, grad_halo[:-1, SEND_MOST:]], axis=0)
    back_upper = jnp.concatenate([grad_halo[1:, :SEND_MOST], empty_grad], axis=0)
    returned = jnp.concatenate([back_lower, back_upper], axis=1)

    def return_rows(values, positions):
        return gather_sum(values, positions, NODES_DEV)
    grad_nodes = grad_own + jax.vmap(return_rows)(returned, send_lists)
    grad_latent = grad_nodes.reshape(FINE_NODES, LATENT).astype(jnp.bfloat16)
    return (updated, grad_latent, totals[0].reshape(-1), totals[1].reshape(-1), totals[2].reshape(-1))
```

```python
from types import SimpleNamespace

import jax
import jax.numpy as jnp
from jax import lax
from jax.experimental import pallas as pl
from jax.experimental.pallas import tpu as pltpu
from jax.sharding import PartitionSpec as P

COARSE_DEV = 8
CORES = 2
EPSILON = 1e-06
VMEM_BYTES = 60 * 1024 * 1024
MESH = pl.DeviceIdType.MESH
BF16, F32, I32 = jnp.bfloat16, jnp.float32, jnp.int32


def nn(a, b):
    return lax.dot_general(a, b, (((1,), (0,)), ((), ())), preferred_element_type=F32)


def nt(a, b):
    return lax.dot_general(a, b, (((1,), (1,)), ((), ())), preferred_element_type=F32)


def tn(a, b):
    return lax.dot_general(a, b, (((0,), (0,)), ((), ())), preferred_element_type=F32)


def iota(shape, dim):
    return lax.broadcasted_iota(I32, shape, dim)


def hot(condition):
    return jnp.where(condition, 1.0, 0.0).astype(BF16)


def one_hot(positions, extent):
    return hot(iota((extent, positions.shape[1]), 0) == positions)


def restriction(ids, weights, extent):
    column = iota((extent, ids.shape[1]), 0)
    first = jnp.where(ids[0:1] == column, weights[0:1], 0.0)
    return first + jnp.where(ids[1:2] == column, weights[1:2], 0.0)


def silu_slope(preact):
    logistic = jax.nn.sigmoid(preact)
    return logistic * (1.0 + preact * (1.0 - logistic))


def mean_last(values):
    return jnp.mean(values, axis=-1, keepdims=True)


def fold(values):
    half = values.shape[1] // 2
    return jnp.concatenate([values[:, :half], values[:, half:]], axis=0)


def unfold(values):
    half = values.shape[0] // 2
    return jnp.concatenate([values[:half], values[half:]], axis=1)


def make_kernel(ny, nz, nx, width, nodes, edges, sends, coarse, cedges):
    half = width // CORES
    sizes = {"y": ny, "z": nz, "x": nx}
    orders = (("x", "z", "y"), ("y", "x", "z"), ("z", "x", "y"))
    table = nodes + nodes + 2 * sends

    def vmem(*shape, kind=BF16):
        return pltpu.VMEM(shape, kind)

    def sems(*count):
        return pltpu.SemaphoreType.DMA(count)

    loaded = dict(
        node=vmem(nodes, width),
        edge=vmem(edges, width),
        cedge=vmem(cedges, width),
        ws=vmem(width, width),
        wt=vmem(width, width),
        wn=vmem(width, width),
        cot=vmem(nodes, width),
        halo=vmem(1, 2, sends, kind=I32),
        src=vmem(1, edges, kind=I32),
        dst=vmem(1, edges, kind=I32),
        csrc=vmem(1, cedges, kind=I32),
        cdst=vmem(1, cedges, kind=I32),
        ids=vmem(2, nodes, kind=I32),
        wts=vmem(2, nodes, kind=F32),
    )
    work = dict(
        oht=vmem(table, edges),
        oh=vmem(edges, table),
        proj=vmem(table, width),
        pre=vmem(edges, width, kind=F32),
        msg=vmem(edges, width),
        normed=vmem(nodes, width, kind=F32),
        fine_out=vmem(nodes, width, kind=F32),
        upd=vmem(nodes, width),
        lat=vmem(nodes, width),
        in_sem=sems(len(loaded)),
        out_sem=sems(5),
    )

    def exchange(out, into, *count):
        return dict(out=out, into=into, ss=sems(*count), rs=sems(*count))

    rows = vmem(2 * sends, width)
    halves = [exchange(rows, rows, 2) for _ in range(2)]
    sums = [exchange(vmem(coarse, width), vmem(nx - 1, coarse, width), nx - 1) for _ in range(2)]
    streams = []
    for i, (a, b, c) in enumerate(orders):
        n1, n2, n3 = sizes[a], sizes[b], sizes[c]
        c1 = half // n1
        c2 = c1 // n2
        first = vmem(half, width)
        second = vmem(n1 - 1, c1, width)
        third = vmem(n2 - 1, 2 * c2, width // 2)
        last = vmem(n3 - 1, 1, width, kind=F32)
        streams.append(
            dict(
                perm=vmem(width, width),
                left=vmem(width, nodes + coarse + (2 * sends if i == 0 else 0)),
                keep=vmem(half, width, kind=F32),
                row=vmem(1, width, kind=F32),
                levels=[
                    exchange(first, first, 1),
                    exchange(second, second, n1 - 1),
                    exchange(third, third, n2 - 1),
                    exchange(last, last, n3 - 1),
                ],
            )
        )
    scratch = [loaded, work, halves, sums, streams]

    def kernel(*refs):
        count = len(loaded)
        given, outs = refs[:count], refs[count : count + 5]
        held, work, halves, sums, streams = refs[count + 5 :]
        v = SimpleNamespace(**held, **work)
        halves, sums = ([SimpleNamespace(**e) for e in group] for group in (halves, sums))
        streams = [SimpleNamespace(**stream) for stream in streams]
        for stream in streams:
            stream.levels = [SimpleNamespace(**level) for level in stream.levels]
        for stream, order in zip(streams, orders):
            stream.order = order
        source_stream, target_stream, node_stream = streams
        halo_rows, back_rows = halves
        cot_sum, val_sum = sums
        dom, x = lax.axis_index("dom"), lax.axis_index("grp")
        core = dom % CORES
        z = (dom // CORES) % nz
        y = dom // (CORES * nz)

        loads = SimpleNamespace(
            **{
                name: pltpu.make_async_copy(ref, held[name], v.in_sem.at[i])
                for i, (name, ref) in enumerate(zip(loaded, given))
            }
        )
        for load in (
            loads.halo,
            loads.node,
            loads.src,
            loads.dst,
            loads.ids,
            loads.wts,
            loads.csrc,
            loads.cdst,
            loads.cot,
            loads.wt,
            loads.ws,
            loads.edge,
            loads.wn,
            loads.cedge,
        ):
            load.start()

        def place(y, z, core, x):
            return ((y * nz + z) * CORES + core, x)

        def line(axis, k):
            if axis == "x":
                return place(y, z, core, (x + k) % nx)
            if axis == "y":
                return place((y + k) % ny, z, core, x)
            return place(y, (z + k) % nz, core, x)

        twin = place(y, z, 1 - core, x)
        total = ny * nz * CORES * nx
        here = dom * nx + x
        above, below = (here + 1) % total, (here + total - 1) % total
        above, below = (above // nx, above % nx), (below // nx, below % nx)

        barrier = pltpu.get_barrier_semaphore()
        partners = [twin, above, below]
        for axis in ("x", "y", "z"):
            partners += [line(axis, k) for k in range(1, sizes[axis])]
        for partner in partners:
            pl.semaphore_signal(barrier, inc=1, device_id=partner, device_id_type=MESH)

        def remote(source, target, send_sem, recv_sem, device):
            return pltpu.make_async_remote_copy(
                src_ref=source,
                dst_ref=target,
                send_sem=send_sem,
                recv_sem=recv_sem,
                device_id=device,
                device_id_type=MESH,
            )

        started = []

        def start(copies):
            for copy in copies:
                copy.start()
            started.extend(copies)
            return copies

        loads.halo.wait()
        lists = v.halo[0]
        side = [one_hot(lists[s : s + 1], nodes) for s in range(2)]
        loads.node.wait()
        node = v.node[...]
        for s in range(2):
            halo_rows.out[s * sends : (s + 1) * sends] = tn(side[s], node).astype(BF16)
        low, high = pl.ds(0, sends), pl.ds(sends, sends)
        loads.ids.wait()
        loads.wts.wait()
        restrict = restriction(v.ids[...], v.wts[...], coarse).astype(BF16)
        loads.cot.wait()
        cot_sum.out[...] = nn(restrict, v.cot[...]).astype(BF16)

        pl.semaphore_wait(barrier, len(partners))

        def to_neighbours(e):
            return start(
                [
                    remote(e.out.at[low], e.into.at[high], e.ss.at[0], e.rs.at[0], below),
                    remote(e.out.at[high], e.into.at[low], e.ss.at[1], e.rs.at[1], above),
                ]
            )

        def to_line(e, axis):
            return start(
                [
                    remote(
                        e.out.at[k - 1],
                        e.into.at[k - 1],
                        e.ss.at[k - 1],
                        e.rs.at[k - 1],
                        line(axis, k),
                    )
                    for k in range(1, sizes[axis])
                ]
            )

        halo = to_neighbours(halo_rows)

        def to_group(e):
            return start(
                [
                    remote(
                        e.out, e.into.at[k - 1], e.ss.at[k - 1], e.rs.at[k - 1], line("x", k)
                    )
                    for k in range(1, nx)
                ]
            )

        def group_sum(e, copies):
            running = e.out[...].astype(F32)
            for k, copy in enumerate(copies):
                copy.wait_recv()
                running = running + e.into[k].astype(F32)
            return running

        cot_copies = to_group(cot_sum)

        loads.src.wait()
        loads.dst.wait()
        v.oht[0:nodes] = one_hot(v.dst[...], nodes)
        v.oht[nodes:] = one_hot(v.src[...], table - nodes)
        eye = hot(iota((edges, edges), 0) == iota((edges, edges), 1))
        v.oh[...] = nt(eye, v.oht[...]).astype(BF16)
        loads.wt.wait()
        v.proj[0:nodes] = nn(node, v.wt[...]).astype(BF16)
        loads.ws.wait()
        v.proj[nodes : 2 * nodes] = nn(node, v.ws[...]).astype(BF16)
        loads.edge.wait()
        chunk = edges // 4
        local = 2 * nodes
        for e in range(0, edges, chunk):
            rows = slice(e, e + chunk)
            v.pre[rows] = v.edge[rows].astype(F32) + nn(
                v.oh[rows, 0:local], v.proj[0:local]
            )
        for copy in halo:
            copy.wait_recv()
        v.proj[local:] = nn(halo_rows.into[...], v.ws[...]).astype(BF16)
        for e in range(0, edges, chunk):
            rows = slice(e, e + chunk)
            preact = v.pre[rows] + nn(v.oh[rows, local:], v.proj[local:])
            v.pre[rows] = preact
            v.msg[rows] = jax.nn.silu(preact).astype(BF16)
        summed = nn(v.oht[0:nodes], v.msg[...])
        inverse = lax.rsqrt(mean_last(summed * summed) + EPSILON)
        normed = summed * inverse
        v.normed[...] = normed
        normed_half = normed.astype(BF16)
        loads.wn.wait()
        fine_out = node.astype(F32) + nn(normed_half, v.wn[...])
        v.fine_out[...] = fine_out
        val_sum.out[...] = nn(restrict, fine_out.astype(BF16)).astype(BF16)
        val_copies = to_group(val_sum)

        for stream, order in zip(streams, orders):
            rest = iota((width, width), 0)
            digits = {}
            for axis in reversed(order):
                digits[axis] = rest % sizes[axis]
                rest = rest // sizes[axis]
            owner_core = jnp.where(rest == 0, 1 - core, core)
            row = ((y + digits["y"]) % ny) * nz + (z + digits["z"]) % nz
            row = (row * CORES + owner_core) * nx + (x + digits["x"]) % nx
            stream.perm[...] = hot(row == iota((width, width), 1))
        source_stream.left[:, 0:nodes] = nt(source_stream.perm[...], node).astype(BF16)
        target_stream.left[:, 0:nodes] = nt(target_stream.perm[...], node).astype(BF16)
        node_stream.left[:, 0:nodes] = nt(node_stream.perm[...], normed_half).astype(BF16)
        for e in range(0, edges, chunk):
            rows = slice(e, e + chunk)
            v.pre[rows] = silu_slope(v.pre[rows])
        loads.csrc.wait()
        loads.cdst.wait()
        coarse_hot_t = jnp.concatenate(
            [one_hot(v.cdst[...], coarse), one_hot(v.csrc[...], coarse)], axis=0
        )
        eye = hot(iota((cedges, cedges), 0) == iota((cedges, cedges), 1))
        coarse_hot = nt(eye, coarse_hot_t).astype(BF16)
        eye = hot(iota((nodes, nodes), 0) == iota((nodes, nodes), 1))
        prolong = nt(eye, restrict).astype(BF16)
        grad_coarse = group_sum(cot_sum, cot_copies)
        grad_coarse_half = grad_coarse.astype(BF16)
        coarse_normed_grad = nt(grad_coarse_half, v.wn[...])
        loads.cedge.wait()
        coarse_edge = v.cedge[...].astype(F32)

        coarse_half = group_sum(val_sum, val_copies).astype(BF16)
        coarse_proj = jnp.concatenate(
            [nn(coarse_half, v.wt[...]), nn(coarse_half, v.ws[...])], axis=0
        ).astype(BF16)
        preact = coarse_edge + nn(coarse_hot, coarse_proj)
        message = jax.nn.silu(preact).astype(BF16)
        summed = nn(coarse_hot_t[0:coarse], message)
        coarse_inverse = lax.rsqrt(mean_last(summed * summed) + EPSILON)
        coarse_normed = summed * coarse_inverse
        coarse_normed_half = coarse_normed.astype(BF16)
        grad_summed = coarse_inverse * (
            coarse_normed_grad - coarse_normed * mean_last(coarse_normed_grad * coarse_normed)
        )
        grad_preact = (
            nn(coarse_hot[:, 0:coarse], grad_summed.astype(BF16)) * silu_slope(preact)
        ).astype(BF16)
        coarse_grad = nn(coarse_hot_t, grad_preact).astype(BF16)
        grad_coarse_in = (
            grad_coarse
            + nt(coarse_grad[coarse:], v.ws[...])
            + nt(coarse_grad[0:coarse], v.wt[...])
        )
        grad_fine = v.cot[...].astype(F32) + nn(prolong, grad_coarse_in.astype(BF16))
        grad_half = grad_fine.astype(BF16)

        mine = (iota((coarse, width), 0) // COARSE_DEV) == x
        own_coarse = jnp.where(mine, coarse_half.astype(F32), 0.0).astype(BF16)
        own_normed = jnp.where(mine, coarse_normed, 0.0).astype(BF16)

        def write(source, index):
            copy = pltpu.make_async_copy(source, outs[index], v.out_sem.at[index])
            copy.start()
            return copy

        def stage0(stream, right):
            e = stream.levels[0]
            e.out[...] = nn(stream.left[0:half], right).astype(BF16)
            copies = start([remote(e.out, e.into, e.ss.at[0], e.rs.at[0], twin)])
            stream.keep[...] = nn(stream.left[half:], right)
            return copies

        def stage1(stream, copies):
            axis = stream.order[0]
            size = half // sizes[axis]
            e, keep = stream.levels[0], stream.keep
            copies[0].wait_recv()
            for k in range(1, sizes[axis]):
                rows = slice(k * size, (k + 1) * size)
                stream.levels[1].out[k - 1] = (keep[rows] + e.into[rows].astype(F32)).astype(BF16)
            sent = to_line(stream.levels[1], axis)
            keep[0:size] = keep[0:size] + e.into[0:size].astype(F32)
            return sent

        def stage2(stream, copies):
            axis = stream.order[1]
            size = half // sizes[stream.order[0]]
            running = stream.keep[0:size]
            for k, copy in enumerate(copies):
                copy.wait_recv()
                running = running + stream.levels[1].into[k].astype(F32)
            size = size // sizes[axis]
            for k in range(1, sizes[axis]):
                part = fold(running[k * size : (k + 1) * size])
                stream.levels[2].out[k - 1] = part.astype(BF16)
            return to_line(stream.levels[2], axis), running[0:size]

        def stage3(stream, state):
            copies, running = state
            axis = stream.order[2]
            for k, copy in enumerate(copies):
                copy.wait_recv()
                running = running + unfold(stream.levels[2].into[k].astype(F32))
            for k in range(1, sizes[axis]):
                stream.levels[3].out[k - 1] = running[k : k + 1]
            return to_line(stream.levels[3], axis), running[0:1]

        def finish(stream, state, index):
            copies, running = state
            for k, copy in enumerate(copies):
                copy.wait_recv()
                running = running + stream.levels[3].into[k]
            stream.row[...] = running
            writes.append(write(stream.row, index))

        node_stream.left[:, nodes:] = nt(node_stream.perm[...], own_normed).astype(BF16)
        node_state = stage0(node_stream, jnp.concatenate([grad_half, grad_coarse_half], axis=0))

        grad_normed = nt(grad_half, v.wn[...])
        normed = v.normed[...]
        grad_summed = inverse * (grad_normed - normed * mean_last(grad_normed * normed))
        grad_summed = grad_summed.astype(BF16)
        for e in range(0, edges, chunk):
            rows = slice(e, e + chunk)
            v.msg[rows] = (nn(v.oh[rows, 0:nodes], grad_summed) * v.pre[rows]).astype(BF16)
        grad_dst = nn(v.oht[0:nodes], v.msg[...]).astype(BF16)
        target_stream.left[:, nodes:] = nt(target_stream.perm[...], own_coarse).astype(BF16)
        target_state = stage0(target_stream, jnp.concatenate([grad_dst, coarse_grad[0:coarse]], axis=0))
        node_state = stage1(node_stream, node_state)
        grad_src = nn(v.oht[nodes:], v.msg[...]).astype(BF16)
        source_stream.left[:, nodes:] = nt(
            source_stream.perm[...], jnp.concatenate([halo_rows.into[...], own_coarse], axis=0)
        ).astype(BF16)
        source_state = stage0(source_stream, jnp.concatenate([grad_src, coarse_grad[coarse:]], axis=0))
        back_rows.out[...] = nt(grad_src[nodes:], v.ws[...]).astype(BF16)
        back = to_neighbours(back_rows)
        target_state = stage1(target_stream, target_state)
        source_state = stage1(source_stream, source_state)
        grad_latent = grad_fine + nt(grad_src[0:nodes], v.ws[...]) + nt(grad_dst, v.wt[...])
        coarse_out = coarse_half.astype(F32) + nn(coarse_normed_half, v.wn[...])
        updated = v.fine_out[...] + nn(prolong, coarse_out.astype(BF16))
        v.upd[...] = updated.astype(BF16)
        writes = [write(v.upd, 0)]
        node_state = stage2(node_stream, node_state)
        for copy in back:
            copy.wait_recv()
        for s in range(2):
            grad_latent = grad_latent + nn(side[s], back_rows.into[s * sends : (s + 1) * sends])
        v.lat[...] = grad_latent.astype(BF16)
        writes.append(write(v.lat, 1))
        node_state = stage3(node_stream, node_state)
        source_state = stage2(source_stream, source_state)
        target_state = stage2(target_stream, target_state)
        finish(node_stream, node_state, 4)
        source_state = stage3(source_stream, source_state)
        target_state = stage3(target_stream, target_state)
        finish(source_stream, source_state, 2)
        finish(target_stream, target_state, 3)
        for copy in started:
            copy.wait_send()
        for copy in writes:
            copy.wait()

    return kernel, scratch


def write_out(*refs):
    count = len(refs) // 2
    sems = refs[-1]
    copies = [pltpu.make_async_copy(refs[i], refs[count + i], sems.at[i]) for i in range(count)]
    for copy in copies:
        copy.start()
    for copy in copies:
        copy.wait()


def solution(mesh):
    nx = mesh.shape["grp"]
    chips = mesh.shape["dom"] // CORES
    ny = 1
    while ny * ny < chips:
        ny += 1
    nz = chips // ny

    def step(node, edge, cedge, ws, wt, wn, cot, halo, src, dst, csrc, cdst, ids, weights):
        nodes, width = node.shape
        kernel, scratch = make_kernel(
            ny,
            nz,
            nx,
            width,
            nodes,
            edge.shape[0],
            halo.shape[2],
            COARSE_DEV * nx,
            cedge.shape[0],
        )
        row = jax.ShapeDtypeStruct((1, width), F32)
        rows = jax.ShapeDtypeStruct((nodes, width), BF16)
        shapes = (rows, rows, row, row, row)
        held = pl.pallas_call(
            kernel,
            out_shape=shapes,
            in_specs=[pl.BlockSpec(memory_space=pltpu.HBM)] * 14,
            out_specs=[pl.BlockSpec(memory_space=pltpu.HBM)] * 5,
            scratch_shapes=scratch,
            compiler_params=pltpu.CompilerParams(
                collective_id=0, has_side_effects=True, vmem_limit_bytes=VMEM_BYTES
            ),
        )(
            node,
            edge,
            cedge,
            ws,
            wt,
            wn,
            cot,
            halo,
            src.reshape(1, -1),
            dst.reshape(1, -1),
            csrc.reshape(1, -1),
            cdst.reshape(1, -1),
            ids,
            weights,
        )
        updated, latent, gs, gt, gn = pl.pallas_call(
            write_out,
            out_shape=shapes,
            in_specs=[pl.BlockSpec(memory_space=pltpu.HBM)] * 5,
            out_specs=[pl.BlockSpec(memory_space=pltpu.HBM)] * 5,
            scratch_shapes=[pltpu.SemaphoreType.DMA((5,))],
            compiler_params=pltpu.CompilerParams(vmem_limit_bytes=VMEM_BYTES),
        )(*held)
        return updated, latent, gs.reshape(-1), gt.reshape(-1), gn.reshape(-1)

    fine = P(("dom", "grp"), None)
    flat = P(("dom", "grp"))
    return jax.shard_map(
        step,
        mesh=mesh,
        in_specs=(
            fine,
            fine,
            P("dom", None),
            P(),
            P(),
            P(),
            fine,
            P(("dom", "grp"), None, None),
            flat,
            flat,
            P("dom"),
            P("dom"),
            P(None, ("dom", "grp")),
            P(None, ("dom", "grp")),
        ),
        out_specs=(fine, fine, flat, flat, flat),
        check_vma=False,
    )
```

```python
from types import SimpleNamespace

import jax
import jax.numpy as jnp
from jax import lax
from jax.experimental import pallas as pl
from jax.experimental.pallas import tpu as pltpu
from jax.sharding import PartitionSpec as P

COARSE_DEV = 8
CORES = 2
EPSILON = 1e-06
VMEM_BYTES = 48 * 1024 * 1024
MESH = pl.DeviceIdType.MESH
BF16, F32, I32 = jnp.bfloat16, jnp.float32, jnp.int32


def nn(a, b):
    return lax.dot_general(a, b, (((1,), (0,)), ((), ())), preferred_element_type=F32)


def nt(a, b):
    return lax.dot_general(a, b, (((1,), (1,)), ((), ())), preferred_element_type=F32)


def tn(a, b):
    return lax.dot_general(a, b, (((0,), (0,)), ((), ())), preferred_element_type=F32)


def iota(shape, dim):
    return lax.broadcasted_iota(I32, shape, dim)


def hot(condition):
    return jnp.where(condition, 1.0, 0.0).astype(BF16)


def one_hot(positions, extent):
    return hot(iota((extent, positions.shape[1]), 0) == positions)


def restriction(ids, weights, extent):
    column = iota((extent, ids.shape[1]), 0)
    first = jnp.where(ids[0:1] == column, weights[0:1], 0.0)
    return first + jnp.where(ids[1:2] == column, weights[1:2], 0.0)


def silu_slope(preact):
    logistic = jax.nn.sigmoid(preact)
    return logistic * (1.0 + preact * (1.0 - logistic))


def mean_last(values):
    return jnp.mean(values, axis=-1, keepdims=True)


def fold(values):
    half = values.shape[1] // 2
    return jnp.concatenate([values[:, :half], values[:, half:]], axis=0)


def unfold(values):
    half = values.shape[0] // 2
    return jnp.concatenate([values[:half], values[half:]], axis=1)


def make_kernel(ny, nz, nx, width, nodes, edges, sends, coarse, cedges):
    half = width // CORES
    sizes = {"y": ny, "z": nz, "x": nx}
    plans = ((("z",), ("x", "y")), (("y",), ("x", "z")), (("x",), ("z",), ("y",)))

    def offsets(axes):
        places = [{}]
        for axis in axes:
            places = [{**place, axis: k} for place in places for k in range(sizes[axis])]
        return places

    def farthest_first(axes):
        places = offsets(axes)

        def hops(slot):
            return sum(min(k, sizes[axis] - k) for axis, k in places[slot].items())

        return sorted(range(1, len(places)), key=hops, reverse=True)
    table = nodes + nodes + 2 * sends
    rounds = max(ny, nz) // 2

    def vmem(*shape, kind=BF16):
        return pltpu.VMEM(shape, kind)

    def sems(*count):
        return pltpu.SemaphoreType.DMA(count)

    loaded = dict(
        node=vmem(nodes, width),
        edge=vmem(edges, width),
        cedge=vmem(cedges, width),
        ws=vmem(width, width),
        wt=vmem(width, width),
        wn=vmem(width, width),
        cot=vmem(nodes, width),
        halo=vmem(1, 2, sends, kind=I32),
        src=vmem(1, edges, kind=I32),
        dst=vmem(1, edges, kind=I32),
        csrc=vmem(1, cedges, kind=I32),
        cdst=vmem(1, cedges, kind=I32),
        ids=vmem(2, nodes, kind=I32),
        wts=vmem(2, nodes, kind=F32),
    )
    work = dict(
        oht=vmem(table, edges),
        oh=vmem(edges, table),
        proj=vmem(table, width),
        pre=vmem(edges, width, kind=F32),
        msg=vmem(edges, width),
        normed=vmem(nodes, width, kind=F32),
        fine_out=vmem(nodes, width, kind=F32),
        in_sem=sems(len(loaded)),
        hello=pltpu.SemaphoreType.REGULAR((rounds,)),
    )

    def exchange(out, into, count):
        return dict(out=out, into=into, ss=sems(count), rs=sems(count))

    rows = vmem(2 * sends, width)
    halves = [exchange(rows, rows, 2) for _ in range(2)]
    sums = [exchange(vmem(coarse, width), vmem(nx - 1, coarse, width), nx - 1) for _ in range(2)]
    streams = []
    for i, plan in enumerate(plans):
        first = vmem(half, width)
        levels = [exchange(first, first, 1)]
        size = half
        for axes in plan:
            count = len(offsets(axes))
            size = size // count
            if axes is plan[-1]:
                buffer = vmem(count - 1, size, width, kind=F32)
            elif axes is plan[0]:
                buffer = vmem(count - 1, size, width)
            else:
                buffer = vmem(count - 1, 2 * size, width // 2)
            levels.append(exchange(buffer, buffer, count - 1))
        streams.append(
            dict(
                perm=vmem(width, width),
                left=vmem(width, nodes + coarse + (2 * sends if i == 0 else 0)),
                keep=vmem(half, width, kind=F32),
                levels=levels,
            )
        )
    scratch = [loaded, work, halves, sums, streams]

    def kernel(*refs):
        count = len(loaded)
        given, outs = refs[:count], refs[count : count + 5]
        held, work, halves, sums, streams = refs[count + 5 :]
        v = SimpleNamespace(**held, **work)
        halves, sums = ([SimpleNamespace(**e) for e in group] for group in (halves, sums))
        streams = [SimpleNamespace(**stream) for stream in streams]
        for stream in streams:
            stream.levels = [SimpleNamespace(**level) for level in stream.levels]
        for stream, plan, row in zip(streams, plans, outs[2:]):
            stream.plan, stream.row = plan, row
        source_stream, target_stream, node_stream = streams
        halo_rows, back_rows = halves
        cot_sum, val_sum = sums
        dom, x = lax.axis_index("dom"), lax.axis_index("grp")
        core = dom % CORES
        z = (dom // CORES) % nz
        y = dom // (CORES * nz)

        loads = SimpleNamespace(
            **{
                name: pltpu.make_async_copy(ref, held[name], v.in_sem.at[i])
                for i, (name, ref) in enumerate(zip(loaded, given))
            }
        )
        for load in (
            loads.halo,
            loads.node,
            loads.src,
            loads.dst,
            loads.ids,
            loads.wts,
            loads.csrc,
            loads.cdst,
            loads.cot,
            loads.wt,
            loads.ws,
            loads.edge,
            loads.wn,
            loads.cedge,
        ):
            load.start()

        def place(y, z, core, x):
            return ((y * nz + z) * CORES + core, x)

        def at(shift):
            return place(
                (y + shift.get("y", 0)) % ny,
                (z + shift.get("z", 0)) % nz,
                core,
                (x + shift.get("x", 0)) % nx,
            )

        twin = place(y, z, 1 - core, x)
        total = ny * nz * CORES * nx
        here = dom * nx + x
        above, below = (here + 1) % total, (here + total - 1) % total
        above, below = (above // nx, above % nx), (below // nx, below % nx)

        barrier = pltpu.get_barrier_semaphore()
        around = [at({"y": 1}), at({"y": ny - 1}), at({"z": 1}), at({"z": nz - 1})]
        partners = [above, below] + [at({"x": k}) for k in range(1, nx)] + around + [twin]
        for partner in partners:
            pl.semaphore_signal(barrier, inc=1, device_id=partner, device_id_type=MESH)

        def tell(step):
            for partner in around:
                pl.semaphore_signal(
                    v.hello.at[step], inc=1, device_id=partner, device_id_type=MESH
                )

        def hear(step):
            pl.semaphore_wait(v.hello.at[step], len(around))

        def remote(source, target, send_sem, recv_sem, device):
            return pltpu.make_async_remote_copy(
                src_ref=source,
                dst_ref=target,
                send_sem=send_sem,
                recv_sem=recv_sem,
                device_id=device,
                device_id_type=MESH,
            )

        started = []

        def settle():
            for copy in started:
                copy.wait_send()
            started.clear()

        def start(copies):
            for copy in copies:
                copy.start()
            started.extend(copies)
            return copies

        loads.halo.wait()
        lists = v.halo[0]
        side = [one_hot(lists[s : s + 1], nodes) for s in range(2)]
        loads.node.wait()
        node = v.node[...]
        for s in range(2):
            halo_rows.out[s * sends : (s + 1) * sends] = tn(side[s], node).astype(BF16)
        low, high = pl.ds(0, sends), pl.ds(sends, sends)
        pl.semaphore_wait(barrier, len(partners))

        def to_neighbours(e):
            return start(
                [
                    remote(e.out.at[low], e.into.at[high], e.ss.at[0], e.rs.at[0], below),
                    remote(e.out.at[high], e.into.at[low], e.ss.at[1], e.rs.at[1], above),
                ]
            )

        def to_peer(e, source, axes, slot):
            copy = remote(
                source, e.into.at[slot - 1], e.ss.at[slot - 1], e.rs.at[slot - 1], at(offsets(axes)[slot])
            )
            return start([copy])[0]

        def to_group(e):
            return [to_peer(e, e.out, ("x",), slot) for slot in farthest_first(("x",))]

        def group_sum(e, copies):
            for copy in copies:
                copy.wait_recv()
            running = e.out[...].astype(F32)
            for k in range(nx - 1):
                running = running + e.into[k].astype(F32)
            return running

        halo = to_neighbours(halo_rows)
        tell(0)
        loads.ids.wait()
        loads.wts.wait()
        restrict = restriction(v.ids[...], v.wts[...], coarse).astype(BF16)
        loads.cot.wait()
        cot_sum.out[...] = nn(restrict, v.cot[...]).astype(BF16)
        cot_copies = to_group(cot_sum)

        loads.src.wait()
        loads.dst.wait()
        v.oht[0:nodes] = one_hot(v.dst[...], nodes)
        v.oht[nodes:] = one_hot(v.src[...], table - nodes)
        eye = hot(iota((edges, edges), 0) == iota((edges, edges), 1))
        v.oh[...] = nt(eye, v.oht[...]).astype(BF16)
        loads.wt.wait()
        v.proj[0:nodes] = nn(node, v.wt[...]).astype(BF16)
        loads.ws.wait()
        v.proj[nodes : 2 * nodes] = nn(node, v.ws[...]).astype(BF16)
        loads.edge.wait()
        chunk = edges // 4
        local = 2 * nodes
        for e in range(0, edges, chunk):
            rows = slice(e, e + chunk)
            v.pre[rows] = v.edge[rows].astype(F32) + nn(
                v.oh[rows, 0:local], v.proj[0:local]
            )
        for copy in halo:
            copy.wait_recv()
        hear(0)
        tell(1)
        v.proj[local:] = nn(halo_rows.into[...], v.ws[...]).astype(BF16)
        for e in range(0, edges, chunk):
            rows = slice(e, e + chunk)
            preact = v.pre[rows] + nn(v.oh[rows, local:], v.proj[local:])
            v.pre[rows] = preact
            v.msg[rows] = jax.nn.silu(preact).astype(BF16)
        summed = nn(v.oht[0:nodes], v.msg[...])
        inverse = lax.rsqrt(mean_last(summed * summed) + EPSILON)
        normed = summed * inverse
        v.normed[...] = normed
        normed_half = normed.astype(BF16)
        loads.wn.wait()
        fine_out = node.astype(F32) + nn(normed_half, v.wn[...])
        v.fine_out[...] = fine_out
        val_sum.out[...] = nn(restrict, fine_out.astype(BF16)).astype(BF16)
        val_copies = to_group(val_sum)

        for stream in streams:
            order = [axis for axes in stream.plan for axis in axes]
            rest = iota((width, width), 0)
            digits = {}
            for axis in reversed(order):
                digits[axis] = rest % sizes[axis]
                rest = rest // sizes[axis]
            owner_core = jnp.where(rest == 0, 1 - core, core)
            row = ((y + digits["y"]) % ny) * nz + (z + digits["z"]) % nz
            row = (row * CORES + owner_core) * nx + (x + digits["x"]) % nx
            stream.perm[...] = hot(row == iota((width, width), 1))
        source_stream.left[:, 0:nodes] = nt(source_stream.perm[...], node).astype(BF16)
        source_stream.left[:, nodes : nodes + 2 * sends] = nt(
            source_stream.perm[...], halo_rows.into[...]
        ).astype(BF16)
        target_stream.left[:, 0:nodes] = nt(target_stream.perm[...], node).astype(BF16)
        node_stream.left[:, 0:nodes] = nt(node_stream.perm[...], normed_half).astype(BF16)
        for e in range(0, edges, chunk):
            rows = slice(e, e + chunk)
            v.pre[rows] = silu_slope(v.pre[rows])
        loads.csrc.wait()
        loads.cdst.wait()
        coarse_hot_t = jnp.concatenate(
            [one_hot(v.cdst[...], coarse), one_hot(v.csrc[...], coarse)], axis=0
        )
        eye = hot(iota((cedges, cedges), 0) == iota((cedges, cedges), 1))
        coarse_hot = nt(eye, coarse_hot_t).astype(BF16)
        eye = hot(iota((nodes, nodes), 0) == iota((nodes, nodes), 1))
        prolong = nt(eye, restrict).astype(BF16)
        grad_coarse = group_sum(cot_sum, cot_copies)
        grad_coarse_half = grad_coarse.astype(BF16)
        coarse_normed_grad = nt(grad_coarse_half, v.wn[...])
        loads.cedge.wait()
        coarse_edge = v.cedge[...].astype(F32)

        hear(1)
        tell(2)
        coarse_half = group_sum(val_sum, val_copies).astype(BF16)
        coarse_proj = jnp.concatenate(
            [nn(coarse_half, v.wt[...]), nn(coarse_half, v.ws[...])], axis=0
        ).astype(BF16)
        preact = coarse_edge + nn(coarse_hot, coarse_proj)
        message = jax.nn.silu(preact).astype(BF16)
        summed = nn(coarse_hot_t[0:coarse], message)
        coarse_inverse = lax.rsqrt(mean_last(summed * summed) + EPSILON)
        coarse_normed = summed * coarse_inverse
        coarse_normed_half = coarse_normed.astype(BF16)
        grad_summed = coarse_inverse * (
            coarse_normed_grad - coarse_normed * mean_last(coarse_normed_grad * coarse_normed)
        )
        grad_preact = (
            nn(coarse_hot[:, 0:coarse], grad_summed.astype(BF16)) * silu_slope(preact)
        ).astype(BF16)
        coarse_grad = nn(coarse_hot_t, grad_preact).astype(BF16)
        grad_coarse_in = (
            grad_coarse
            + nt(coarse_grad[coarse:], v.ws[...])
            + nt(coarse_grad[0:coarse], v.wt[...])
        )
        grad_fine = v.cot[...].astype(F32) + nn(prolong, grad_coarse_in.astype(BF16))
        grad_half = grad_fine.astype(BF16)

        mine = (iota((coarse, width), 0) // COARSE_DEV) == x
        own_coarse = jnp.where(mine, coarse_half.astype(F32), 0.0).astype(BF16)
        own_normed = jnp.where(mine, coarse_normed, 0.0).astype(BF16)

        def stage0(stream, right):
            e = stream.levels[0]
            e.out[...] = nn(stream.left[0:half], right).astype(BF16)
            copies = start([remote(e.out, e.into, e.ss.at[0], e.rs.at[0], twin)])
            stream.keep[...] = nn(stream.left[half:], right)
            return copies

        def stage1(stream, copies):
            axes = stream.plan[0]
            size = half // len(offsets(axes))
            e, keep, into = stream.levels[1], stream.keep, stream.levels[0].into
            copies[0].wait_recv()
            sent = []
            for slot in farthest_first(axes):
                rows = slice(slot * size, (slot + 1) * size)
                e.out[slot - 1] = (keep[rows] + into[rows].astype(F32)).astype(BF16)
                sent.append(to_peer(e, e.out.at[slot - 1], axes, slot))
            keep[0:size] = keep[0:size] + into[0:size].astype(F32)
            return sent

        def received1(stream, copies):
            size = half // len(offsets(stream.plan[0]))
            running = stream.keep[0:size]
            for copy in reversed(copies):
                copy.wait_recv()
            for k in range(len(copies)):
                running = running + stream.levels[1].into[k].astype(F32)
            return running

        def stage2(stream, copies):
            axes = stream.plan[1]
            running = received1(stream, copies)
            size = running.shape[0] // len(offsets(axes))
            e, sent = stream.levels[2], []
            for slot in farthest_first(axes):
                part = fold(running[slot * size : (slot + 1) * size])
                e.out[slot - 1] = part.astype(BF16)
                sent.append(to_peer(e, e.out.at[slot - 1], axes, slot))
            return sent, running[0:size]

        def received2(stream, state):
            copies, running = state
            for copy in reversed(copies):
                copy.wait_recv()
            for k in range(len(copies)):
                running = running + unfold(stream.levels[2].into[k].astype(F32))
            return running

        def last(stream, running):
            e, axes, sent = stream.levels[-1], stream.plan[-1], []
            for slot in farthest_first(axes):
                e.out[slot - 1] = running[slot : slot + 1]
                sent.append(to_peer(e, e.out.at[slot - 1], axes, slot))
            return sent, running[0:1]

        def finish(stream, state):
            copies, running = state
            for copy in reversed(copies):
                copy.wait_recv()
            stream.row[...] = running + jnp.sum(stream.levels[-1].into[...], axis=0)

        hear(2)
        tell(3)
        node_stream.left[:, nodes:] = nt(node_stream.perm[...], own_normed).astype(BF16)
        node_state = stage0(node_stream, jnp.concatenate([grad_half, grad_coarse_half], axis=0))

        grad_normed = nt(grad_half, v.wn[...])
        normed = v.normed[...]
        grad_summed = inverse * (grad_normed - normed * mean_last(grad_normed * normed))
        grad_summed = grad_summed.astype(BF16)
        for e in range(0, edges, chunk):
            rows = slice(e, e + chunk)
            v.msg[rows] = (nn(v.oh[rows, 0:nodes], grad_summed) * v.pre[rows]).astype(BF16)
        grad_dst = nn(v.oht[0:nodes], v.msg[...]).astype(BF16)
        target_stream.left[:, nodes:] = nt(target_stream.perm[...], own_coarse).astype(BF16)
        target_state = stage0(target_stream, jnp.concatenate([grad_dst, coarse_grad[0:coarse]], axis=0))
        hear(3)
        node_state = stage1(node_stream, node_state)
        grad_src = nn(v.oht[nodes:], v.msg[...]).astype(BF16)
        source_stream.left[:, nodes + 2 * sends :] = nt(source_stream.perm[...], own_coarse).astype(
            BF16
        )
        source_state = stage0(source_stream, jnp.concatenate([grad_src, coarse_grad[coarse:]], axis=0))
        back_rows.out[...] = nt(grad_src[nodes:], v.ws[...]).astype(BF16)
        back = to_neighbours(back_rows)
        target_state = stage1(target_stream, target_state)
        source_state = stage1(source_stream, source_state)
        grad_latent = grad_fine + nt(grad_src[0:nodes], v.ws[...]) + nt(grad_dst, v.wt[...])
        coarse_out = coarse_half.astype(F32) + nn(coarse_normed_half, v.wn[...])
        updated = v.fine_out[...] + nn(prolong, coarse_out.astype(BF16))
        outs[0][...] = updated.astype(BF16)
        node_state = stage2(node_stream, node_state)
        for copy in back:
            copy.wait_recv()
        for s in range(2):
            grad_latent = grad_latent + nn(side[s], back_rows.into[s * sends : (s + 1) * sends])
        outs[1][...] = grad_latent.astype(BF16)
        node_state = last(node_stream, received2(node_stream, node_state))
        target_state = last(target_stream, received1(target_stream, target_state))
        source_state = last(source_stream, received1(source_stream, source_state))
        settle()
        finish(node_stream, node_state)
        finish(target_stream, target_state)
        finish(source_stream, source_state)

    return kernel, scratch


def write_out(*refs):
    count = len(refs) // 2
    sems = refs[-1]
    copies = [pltpu.make_async_copy(refs[i], refs[count + i], sems.at[i]) for i in range(count)]
    for copy in copies:
        copy.start()
    for copy in copies:
        copy.wait()


def solution(mesh):
    nx = mesh.shape["grp"]
    chips = mesh.shape["dom"] // CORES
    ny = 1
    while ny * ny < chips:
        ny += 1
    nz = chips // ny

    def step(node, edge, cedge, ws, wt, wn, cot, halo, src, dst, csrc, cdst, ids, weights):
        nodes, width = node.shape
        kernel, scratch = make_kernel(
            ny,
            nz,
            nx,
            width,
            nodes,
            edge.shape[0],
            halo.shape[2],
            COARSE_DEV * nx,
            cedge.shape[0],
        )
        row = jax.ShapeDtypeStruct((1, width), F32)
        rows = jax.ShapeDtypeStruct((nodes, width), BF16)
        shapes = (rows, rows, row, row, row)
        lists = [given.reshape(1, -1) for given in (src, dst, csrc, cdst)]
        arguments = (node, edge, cedge, ws, wt, wn, cot, halo, *lists, ids, weights)
        held = pl.pallas_call(
            kernel,
            out_shape=tuple(pltpu.VMEM(shape.shape, shape.dtype) for shape in shapes),
            in_specs=[pl.BlockSpec(memory_space=pltpu.HBM)] * 14,
            out_specs=[pl.BlockSpec(memory_space=pltpu.VMEM)] * 5,
            scratch_shapes=scratch,
            compiler_params=pltpu.CompilerParams(
                collective_id=0, has_side_effects=True, vmem_limit_bytes=VMEM_BYTES
            ),
        )(*(pltpu.with_memory_space_constraint(given, pltpu.HBM) for given in arguments))
        updated, latent, gs, gt, gn = pl.pallas_call(
            write_out,
            out_shape=shapes,
            in_specs=[pl.BlockSpec(memory_space=pltpu.VMEM)] * 5,
            out_specs=[pl.BlockSpec(memory_space=pltpu.HBM)] * 5,
            scratch_shapes=[pltpu.SemaphoreType.DMA((5,))],
            compiler_params=pltpu.CompilerParams(vmem_limit_bytes=VMEM_BYTES),
        )(*held)
        return updated, latent, gs.reshape(-1), gt.reshape(-1), gn.reshape(-1)

    fine = P(("dom", "grp"), None)
    flat = P(("dom", "grp"))
    return jax.shard_map(
        step,
        mesh=mesh,
        in_specs=(
            fine,
            fine,
            P("dom", None),
            P(),
            P(),
            P(),
            fine,
            P(("dom", "grp"), None, None),
            flat,
            flat,
            P("dom"),
            P("dom"),
            P(None, ("dom", "grp")),
            P(None, ("dom", "grp")),
        ),
        out_specs=(fine, fine, flat, flat, flat),
        check_vma=False,
    )
```

```python
from types import SimpleNamespace

import jax
import jax.numpy as jnp
from jax import lax
from jax.experimental import pallas as pl
from jax.experimental.pallas import tpu as pltpu
from jax.sharding import PartitionSpec as P

COARSE_DEV = 8
CORES = 2
EPSILON = 1e-06
VMEM_BYTES = 48 * 1024 * 1024
MESH = pl.DeviceIdType.MESH
BF16, F32, I32 = jnp.bfloat16, jnp.float32, jnp.int32


def nn(a, b):
    return lax.dot_general(a, b, (((1,), (0,)), ((), ())), preferred_element_type=F32)


def nt(a, b):
    return lax.dot_general(a, b, (((1,), (1,)), ((), ())), preferred_element_type=F32)


def tn(a, b):
    return lax.dot_general(a, b, (((0,), (0,)), ((), ())), preferred_element_type=F32)


def iota(shape, dim):
    return lax.broadcasted_iota(I32, shape, dim)


def hot(condition):
    return jnp.where(condition, 1.0, 0.0).astype(BF16)


def one_hot(positions, extent):
    return hot(iota((extent, positions.shape[1]), 0) == positions)


def restriction(ids, weights, extent):
    column = iota((extent, ids.shape[1]), 0)
    first = jnp.where(ids[0:1] == column, weights[0:1], 0.0)
    return first + jnp.where(ids[1:2] == column, weights[1:2], 0.0)


def silu_slope(preact):
    logistic = jax.nn.sigmoid(preact)
    return logistic * (1.0 + preact * (1.0 - logistic))


def mean_last(values):
    return jnp.mean(values, axis=-1, keepdims=True)


def fold(values):
    half = values.shape[1] // 2
    return jnp.concatenate([values[:, :half], values[:, half:]], axis=0)


def unfold(values):
    half = values.shape[0] // 2
    return jnp.concatenate([values[:half], values[half:]], axis=1)


def make_kernel(ny, nz, nx, width, nodes, edges, sends, coarse, cedges):
    half = width // CORES
    sizes = {"y": ny, "z": nz, "x": nx}
    plans = ((("z",), ("x", "y")), (("y",), ("x", "z")), (("x",), ("z",), ("y",)))

    def offsets(axes):
        places = [{}]
        for axis in axes:
            places = [{**place, axis: k} for place in places for k in range(sizes[axis])]
        return places

    def farthest_first(axes):
        places = offsets(axes)

        def hops(slot):
            return sum(min(k, sizes[axis] - k) for axis, k in places[slot].items())

        return sorted(range(1, len(places)), key=hops, reverse=True)
    table = nodes + nodes + 2 * sends
    reach, hops = 2, [1]
    while reach < max(ny, nz) // 2:
        hops.append(2)
        reach += 2
    hops.append(1)

    def vmem(*shape, kind=BF16):
        return pltpu.VMEM(shape, kind)

    def sems(*count):
        return pltpu.SemaphoreType.DMA(count)

    loaded = dict(
        node=vmem(nodes, width),
        edge=vmem(edges, width),
        cedge=vmem(cedges, width),
        ws=vmem(width, width),
        wt=vmem(width, width),
        wn=vmem(width, width),
        cot=vmem(nodes, width),
        halo=vmem(1, 2, sends, kind=I32),
        src=vmem(1, edges, kind=I32),
        dst=vmem(1, edges, kind=I32),
        csrc=vmem(1, cedges, kind=I32),
        cdst=vmem(1, cedges, kind=I32),
        ids=vmem(2, nodes, kind=I32),
        wts=vmem(2, nodes, kind=F32),
    )
    work = dict(
        oht=vmem(table, edges),
        oh=vmem(edges, table),
        proj=vmem(table, width),
        pre=vmem(edges, width, kind=F32),
        msg=vmem(edges, width),
        normed=vmem(nodes, width, kind=F32),
        fine_out=vmem(nodes, width, kind=F32),
        in_sem=sems(len(loaded)),
        hello=pltpu.SemaphoreType.REGULAR((len(hops),)),
    )

    def exchange(out, into, count):
        return dict(out=out, into=into, ss=sems(count), rs=sems(count))

    rows = vmem(2 * sends, width)
    halves = [exchange(rows, rows, 2) for _ in range(2)]
    sums = [exchange(vmem(coarse, width), vmem(nx - 1, coarse, width), nx - 1) for _ in range(2)]
    streams = []
    for i, plan in enumerate(plans):
        first = vmem(half, width)
        levels = [exchange(first, first, 1)]
        size = half
        for axes in plan:
            count = len(offsets(axes))
            size = size // count
            if axes is plan[-1]:
                buffer = vmem(count - 1, size, width, kind=F32)
            elif axes is plan[0]:
                buffer = vmem(count - 1, size, width)
            else:
                buffer = vmem(count - 1, 2 * size, width // 2)
            levels.append(exchange(buffer, buffer, count - 1))
        streams.append(
            dict(
                perm=vmem(width, width),
                left=vmem(width, nodes + coarse + (2 * sends if i == 0 else 0)),
                keep=vmem(half, width, kind=F32),
                levels=levels,
            )
        )
    scratch = [loaded, work, halves, sums, streams]

    def kernel(*refs):
        count = len(loaded)
        given, outs = refs[:count], refs[count : count + 5]
        held, work, halves, sums, streams = refs[count + 5 :]
        v = SimpleNamespace(**held, **work)
        halves, sums = ([SimpleNamespace(**e) for e in group] for group in (halves, sums))
        streams = [SimpleNamespace(**stream) for stream in streams]
        for stream in streams:
            stream.levels = [SimpleNamespace(**level) for level in stream.levels]
        for stream, plan, row in zip(streams, plans, outs[2:]):
            stream.plan, stream.row = plan, row
        source_stream, target_stream, node_stream = streams
        halo_rows, back_rows = halves
        cot_sum, val_sum = sums
        dom, x = lax.axis_index("dom"), lax.axis_index("grp")
        core = lax.rem(dom, CORES)
        z = lax.rem(lax.div(dom, CORES), nz)
        y = lax.div(dom, CORES * nz)
        ring = dict(
            x=[x] + [lax.rem(x + k, nx) for k in range(1, nx)],
            y=[y] + [lax.rem(y + k, ny) for k in range(1, ny)],
            z=[z] + [lax.rem(z + k, nz) for k in range(1, nz)],
        )

        loads = SimpleNamespace(
            **{
                name: pltpu.make_async_copy(ref, held[name], v.in_sem.at[i])
                for i, (name, ref) in enumerate(zip(loaded, given))
            }
        )

        def place(y, z, core, x):
            return ((y * nz + z) * CORES + core, x)

        def at(shift):
            return place(
                ring["y"][shift.get("y", 0)],
                ring["z"][shift.get("z", 0)],
                core,
                ring["x"][shift.get("x", 0)],
            )

        twin = place(y, z, 1 - core, x)
        total = ny * nz * CORES * nx
        here = dom * nx + x
        above, below = lax.rem(here + 1, total), lax.rem(here + total - 1, total)
        above, below = ((lax.div(n, nx), lax.rem(n, nx)) for n in (above, below))

        barrier = pltpu.get_barrier_semaphore()
        around = [at({"y": 1}), at({"y": ny - 1}), at({"z": 1}), at({"z": nz - 1})]
        partners = [above, below] + [at({"x": k}) for k in range(1, nx)] + around + [twin]
        for partner in partners:
            pl.semaphore_signal(barrier, inc=1, device_id=partner, device_id_type=MESH)

        for load in (
            loads.halo,
            loads.node,
            loads.src,
            loads.dst,
            loads.ids,
            loads.wts,
            loads.csrc,
            loads.cdst,
            loads.cot,
            loads.wt,
            loads.ws,
            loads.edge,
            loads.wn,
            loads.cedge,
        ):
            load.start()

        def tell(step):
            hop = hops[step]
            for shift in ({"y": hop}, {"y": ny - hop}, {"z": hop}, {"z": nz - hop}):
                pl.semaphore_signal(
                    v.hello.at[step], inc=1, device_id=at(shift), device_id_type=MESH
                )

        def hear(step):
            pl.semaphore_wait(v.hello.at[step], len(around))

        def remote(source, target, send_sem, recv_sem, device):
            return pltpu.make_async_remote_copy(
                src_ref=source,
                dst_ref=target,
                send_sem=send_sem,
                recv_sem=recv_sem,
                device_id=device,
                device_id_type=MESH,
            )

        started = []

        def settle():
            for copy in started:
                copy.wait_send()
            started.clear()

        def start(copies):
            for copy in copies:
                copy.start()
            started.extend(copies)
            return copies

        loads.halo.wait()
        lists = v.halo[0]
        side = [one_hot(lists[s : s + 1], nodes) for s in range(2)]
        loads.node.wait()
        node = v.node[...]
        for s in range(2):
            halo_rows.out[s * sends : (s + 1) * sends] = tn(side[s], node).astype(BF16)
        low, high = pl.ds(0, sends), pl.ds(sends, sends)
        pl.semaphore_wait(barrier, len(partners))

        def to_neighbours(e):
            return start(
                [
                    remote(e.out.at[low], e.into.at[high], e.ss.at[0], e.rs.at[0], below),
                    remote(e.out.at[high], e.into.at[low], e.ss.at[1], e.rs.at[1], above),
                ]
            )

        def to_peer(e, source, axes, slot):
            copy = remote(
                source, e.into.at[slot - 1], e.ss.at[slot - 1], e.rs.at[slot - 1], at(offsets(axes)[slot])
            )
            return start([copy])[0]

        def to_group(e):
            return [to_peer(e, e.out, ("x",), slot) for slot in farthest_first(("x",))]

        def group_sum(e, copies):
            for copy in copies:
                copy.wait_recv()
            running = e.out[...].astype(F32)
            for k in range(nx - 1):
                running = running + e.into[k].astype(F32)
            return running

        halo = to_neighbours(halo_rows)
        tell(0)
        loads.ids.wait()
        loads.wts.wait()
        restrict = restriction(v.ids[...], v.wts[...], coarse).astype(BF16)
        loads.cot.wait()
        cot_sum.out[...] = nn(restrict, v.cot[...]).astype(BF16)
        cot_copies = to_group(cot_sum)

        loads.src.wait()
        loads.dst.wait()
        v.oht[0:nodes] = one_hot(v.dst[...], nodes)
        v.oht[nodes:] = one_hot(v.src[...], table - nodes)
        eye = hot(iota((edges, edges), 0) == iota((edges, edges), 1))
        v.oh[...] = nt(eye, v.oht[...]).astype(BF16)
        loads.wt.wait()
        v.proj[0:nodes] = nn(node, v.wt[...]).astype(BF16)
        loads.ws.wait()
        v.proj[nodes : 2 * nodes] = nn(node, v.ws[...]).astype(BF16)
        loads.edge.wait()
        chunk = edges // 4
        local = 2 * nodes
        for e in range(0, edges, chunk):
            rows = slice(e, e + chunk)
            v.pre[rows] = v.edge[rows].astype(F32) + nn(
                v.oh[rows, 0:local], v.proj[0:local]
            )
        for copy in halo:
            copy.wait_recv()
        hear(0)
        tell(1)
        v.proj[local:] = nn(halo_rows.into[...], v.ws[...]).astype(BF16)
        for e in range(0, edges, chunk):
            rows = slice(e, e + chunk)
            preact = v.pre[rows] + nn(v.oh[rows, local:], v.proj[local:])
            v.pre[rows] = preact
            v.msg[rows] = jax.nn.silu(preact).astype(BF16)
        summed = nn(v.oht[0:nodes], v.msg[...])
        inverse = lax.rsqrt(mean_last(summed * summed) + EPSILON)
        normed = summed * inverse
        v.normed[...] = normed
        normed_half = normed.astype(BF16)
        loads.wn.wait()
        fine_out = node.astype(F32) + nn(normed_half, v.wn[...])
        v.fine_out[...] = fine_out
        val_sum.out[...] = nn(restrict, fine_out.astype(BF16)).astype(BF16)
        val_copies = to_group(val_sum)

        for stream in streams:
            order = [axis for axes in stream.plan for axis in axes]
            rest = iota((width, width), 0)
            digits = {}
            for axis in reversed(order):
                digits[axis] = rest % sizes[axis]
                rest = rest // sizes[axis]
            owner_core = jnp.where(rest == 0, 1 - core, core)
            row = ((y + digits["y"]) % ny) * nz + (z + digits["z"]) % nz
            row = (row * CORES + owner_core) * nx + (x + digits["x"]) % nx
            stream.perm[...] = hot(row == iota((width, width), 1))
        source_stream.left[:, 0:nodes] = nt(source_stream.perm[...], node).astype(BF16)
        source_stream.left[:, nodes : nodes + 2 * sends] = nt(
            source_stream.perm[...], halo_rows.into[...]
        ).astype(BF16)
        target_stream.left[:, 0:nodes] = nt(target_stream.perm[...], node).astype(BF16)
        node_stream.left[:, 0:nodes] = nt(node_stream.perm[...], normed_half).astype(BF16)
        for stream in streams:
            stream.left[:, -coarse:] = jnp.zeros((width, coarse), BF16)
        for e in range(0, edges, chunk):
            rows = slice(e, e + chunk)
            v.pre[rows] = silu_slope(v.pre[rows])
        loads.csrc.wait()
        loads.cdst.wait()
        coarse_hot_t = jnp.concatenate(
            [one_hot(v.cdst[...], coarse), one_hot(v.csrc[...], coarse)], axis=0
        )
        eye = hot(iota((cedges, cedges), 0) == iota((cedges, cedges), 1))
        coarse_hot = nt(eye, coarse_hot_t).astype(BF16)
        eye = hot(iota((nodes, nodes), 0) == iota((nodes, nodes), 1))
        prolong = nt(eye, restrict).astype(BF16)
        grad_coarse = group_sum(cot_sum, cot_copies)
        grad_coarse_half = grad_coarse.astype(BF16)
        coarse_normed_grad = nt(grad_coarse_half, v.wn[...])
        loads.cedge.wait()
        coarse_edge = v.cedge[...].astype(F32)

        for step in range(1, len(hops) - 1):
            hear(step)
            tell(step + 1)
        coarse_half = group_sum(val_sum, val_copies).astype(BF16)
        coarse_proj = jnp.concatenate(
            [nn(coarse_half, v.wt[...]), nn(coarse_half, v.ws[...])], axis=0
        ).astype(BF16)
        quarter = width // nx
        rows = pl.ds(pl.multiple_of(x * quarter, quarter), quarter)
        preact = coarse_edge + nn(coarse_hot, coarse_proj)
        target_stream.left[rows, nodes:] = nt(target_stream.perm[rows], coarse_half).astype(BF16)
        source_stream.left[rows, nodes + 2 * sends :] = nt(
            source_stream.perm[rows], coarse_half
        ).astype(BF16)
        message = jax.nn.silu(preact).astype(BF16)
        summed = nn(coarse_hot_t[0:coarse], message)
        coarse_inverse = lax.rsqrt(mean_last(summed * summed) + EPSILON)
        coarse_normed = summed * coarse_inverse
        coarse_normed_half = coarse_normed.astype(BF16)
        for begin in range(0, width, half):
            rows = slice(begin, begin + half // nx)
            node_stream.left[rows, nodes:] = nt(node_stream.perm[rows], coarse_normed_half).astype(
                BF16
            )
        grad_summed = coarse_inverse * (
            coarse_normed_grad - coarse_normed * mean_last(coarse_normed_grad * coarse_normed)
        )
        grad_preact = (
            nn(coarse_hot[:, 0:coarse], grad_summed.astype(BF16)) * silu_slope(preact)
        ).astype(BF16)
        coarse_grad = nn(coarse_hot_t, grad_preact).astype(BF16)
        grad_coarse_in = (
            grad_coarse
            + nt(coarse_grad[coarse:], v.ws[...])
            + nt(coarse_grad[0:coarse], v.wt[...])
        )
        grad_fine = v.cot[...].astype(F32) + nn(prolong, grad_coarse_in.astype(BF16))
        grad_half = grad_fine.astype(BF16)

        def stage0(stream, right):
            e = stream.levels[0]
            e.out[...] = nn(stream.left[0:half], right).astype(BF16)
            copies = start([remote(e.out, e.into, e.ss.at[0], e.rs.at[0], twin)])
            return copies

        def stage0_own(stream, right):
            stream.keep[...] = nn(stream.left[half:], right)

        def stage1(stream, copies):
            axes = stream.plan[0]
            size = half // len(offsets(axes))
            e, keep, into = stream.levels[1], stream.keep, stream.levels[0].into
            copies[0].wait_recv()
            sent = []
            for slot in farthest_first(axes):
                rows = slice(slot * size, (slot + 1) * size)
                e.out[slot - 1] = (keep[rows] + into[rows].astype(F32)).astype(BF16)
                sent.append(to_peer(e, e.out.at[slot - 1], axes, slot))
            keep[0:size] = keep[0:size] + into[0:size].astype(F32)
            return sent

        def received1(stream, copies):
            size = half // len(offsets(stream.plan[0]))
            running = stream.keep[0:size]
            for slot, copy in zip(reversed(farthest_first(stream.plan[0])), reversed(copies)):
                copy.wait_recv()
                running = running + stream.levels[1].into[slot - 1].astype(F32)
            return running

        def stage2(stream, copies):
            axes = stream.plan[1]
            running = received1(stream, copies)
            size = running.shape[0] // len(offsets(axes))
            e, sent = stream.levels[2], []
            for slot in farthest_first(axes):
                part = fold(running[slot * size : (slot + 1) * size])
                e.out[slot - 1] = part.astype(BF16)
                sent.append(to_peer(e, e.out.at[slot - 1], axes, slot))
            return sent, running[0:size]

        def received2(stream, state):
            copies, running = state
            for copy in reversed(copies):
                copy.wait_recv()
            for k in range(len(copies)):
                running = running + unfold(stream.levels[2].into[k].astype(F32))
            return running

        def last(stream, running, slots):
            e, axes, sent = stream.levels[-1], stream.plan[-1], []
            for slot in slots:
                e.out[slot - 1] = running[slot : slot + 1]
                sent.append(to_peer(e, e.out.at[slot - 1], axes, slot))
            return sent

        def halved(slots):
            middle = len(slots) // 2
            return slots[:middle], slots[middle:]

        def finish(stream, copies, running):
            for copy in reversed(copies):
                copy.wait_recv()
            stream.row[...] = running[0:1] + jnp.sum(stream.levels[-1].into[...], axis=0)

        right = jnp.concatenate([grad_half, grad_coarse_half], axis=0)
        node_state = stage0(node_stream, right)
        stage0_own(node_stream, right)

        grad_normed = nt(grad_half, v.wn[...])
        normed = v.normed[...]
        grad_summed = inverse * (grad_normed - normed * mean_last(grad_normed * normed))
        grad_summed = grad_summed.astype(BF16)
        for e in range(0, edges, chunk):
            rows = slice(e, e + chunk)
            v.msg[rows] = (nn(v.oh[rows, 0:nodes], grad_summed) * v.pre[rows]).astype(BF16)
        scattered = nn(v.oht[...], v.msg[...]).astype(BF16)
        grad_dst, grad_src = scattered[0:nodes], scattered[nodes:]
        target_right = jnp.concatenate([grad_dst, coarse_grad[0:coarse]], axis=0)
        target_state = stage0(target_stream, target_right)
        source_right = jnp.concatenate([grad_src, coarse_grad[coarse:]], axis=0)
        source_state = stage0(source_stream, source_right)
        node_state = stage1(node_stream, node_state)
        stage0_own(target_stream, target_right)
        stage0_own(source_stream, source_right)
        target_state = stage1(target_stream, target_state)
        source_state = stage1(source_stream, source_state)
        back_rows.out[...] = nt(grad_src[nodes:], v.ws[...]).astype(BF16)
        back = to_neighbours(back_rows)
        grad_latent = grad_fine + nt(grad_src[0:nodes], v.ws[...]) + nt(grad_dst, v.wt[...])
        coarse_out = coarse_half.astype(F32) + nn(coarse_normed_half, v.wn[...])
        updated = v.fine_out[...] + nn(prolong, coarse_out.astype(BF16))
        outs[0][...] = updated.astype(BF16)
        node_state = stage2(node_stream, node_state)
        for copy in back:
            copy.wait_recv()
        for s in range(2):
            grad_latent = grad_latent + nn(side[s], back_rows.into[s * sends : (s + 1) * sends])
        outs[1][...] = grad_latent.astype(BF16)
        target_far, target_near = halved(farthest_first(target_stream.plan[-1]))
        source_far, source_near = halved(farthest_first(source_stream.plan[-1]))
        hear(len(hops) - 1)
        target_sum = received1(target_stream, target_state)
        target_state = last(target_stream, target_sum, target_far)
        source_sum = received1(source_stream, source_state)
        source_state = last(source_stream, source_sum, source_far)
        node_sum = received2(node_stream, node_state)
        node_state = last(node_stream, node_sum, farthest_first(node_stream.plan[-1]))
        target_state += last(target_stream, target_sum, target_near)
        source_state += last(source_stream, source_sum, source_near)
        settle()
        finish(node_stream, node_state, node_sum)
        finish(target_stream, target_state, target_sum)
        finish(source_stream, source_state, source_sum)

    return kernel, scratch


def write_out(*refs):
    count = len(refs) // 2
    sems = refs[-1]
    copies = [pltpu.make_async_copy(refs[i], refs[count + i], sems.at[i]) for i in range(count)]
    for copy in copies:
        copy.start()
    for copy in copies:
        copy.wait()


def solution(mesh):
    nx = mesh.shape["grp"]
    chips = mesh.shape["dom"] // CORES
    ny = 1
    while ny * ny < chips:
        ny += 1
    nz = chips // ny

    def step(node, edge, cedge, ws, wt, wn, cot, halo, src, dst, csrc, cdst, ids, weights):
        nodes, width = node.shape
        kernel, scratch = make_kernel(
            ny,
            nz,
            nx,
            width,
            nodes,
            edge.shape[0],
            halo.shape[2],
            COARSE_DEV * nx,
            cedge.shape[0],
        )
        row = jax.ShapeDtypeStruct((1, width), F32)
        rows = jax.ShapeDtypeStruct((nodes, width), BF16)
        shapes = (rows, rows, row, row, row)
        lists = [given.reshape(1, -1) for given in (src, dst, csrc, cdst)]
        arguments = (node, edge, cedge, ws, wt, wn, cot, halo, *lists, ids, weights)
        held = pl.pallas_call(
            kernel,
            out_shape=tuple(pltpu.VMEM(shape.shape, shape.dtype) for shape in shapes),
            in_specs=[pl.BlockSpec(memory_space=pltpu.HBM)] * 14,
            out_specs=[pl.BlockSpec(memory_space=pltpu.VMEM)] * 5,
            scratch_shapes=scratch,
            compiler_params=pltpu.CompilerParams(
                collective_id=0, has_side_effects=True, vmem_limit_bytes=VMEM_BYTES
            ),
        )(*(pltpu.with_memory_space_constraint(given, pltpu.HBM) for given in arguments))
        updated, latent, gs, gt, gn = pl.pallas_call(
            write_out,
            out_shape=shapes,
            in_specs=[pl.BlockSpec(memory_space=pltpu.VMEM)] * 5,
            out_specs=[pl.BlockSpec(memory_space=pltpu.HBM)] * 5,
            scratch_shapes=[pltpu.SemaphoreType.DMA((5,))],
            compiler_params=pltpu.CompilerParams(vmem_limit_bytes=VMEM_BYTES),
        )(*held)
        return updated, latent, gs.reshape(-1), gt.reshape(-1), gn.reshape(-1)

    fine = P(("dom", "grp"), None)
    flat = P(("dom", "grp"))
    return jax.shard_map(
        step,
        mesh=mesh,
        in_specs=(
            fine,
            fine,
            P("dom", None),
            P(),
            P(),
            P(),
            fine,
            P(("dom", "grp"), None, None),
            flat,
            flat,
            P("dom"),
            P("dom"),
            P(None, ("dom", "grp")),
            P(None, ("dom", "grp")),
        ),
        out_specs=(fine, fine, flat, flat, flat),
        check_vma=False,
    )
```

```python
from types import SimpleNamespace

import jax
import jax.numpy as jnp
from jax import lax
from jax.experimental import pallas as pl
from jax.experimental.pallas import tpu as pltpu
from jax.sharding import PartitionSpec as P

COARSE_DEV = 8
CORES = 2
EPSILON = 1e-06
VMEM_BYTES = 48 * 1024 * 1024
MESH = pl.DeviceIdType.MESH
BF16, F32, I32 = jnp.bfloat16, jnp.float32, jnp.int32


def nn(a, b):
    return lax.dot_general(a, b, (((1,), (0,)), ((), ())), preferred_element_type=F32)


def nt(a, b):
    return lax.dot_general(a, b, (((1,), (1,)), ((), ())), preferred_element_type=F32)


def tn(a, b):
    return lax.dot_general(a, b, (((0,), (0,)), ((), ())), preferred_element_type=F32)


def iota(shape, dim):
    return lax.broadcasted_iota(I32, shape, dim)


def hot(condition):
    return jnp.where(condition, 1.0, 0.0).astype(BF16)


def one_hot(positions, extent):
    return hot(iota((extent, positions.shape[1]), 0) == positions)


def restriction(ids, weights, extent):
    column = iota((extent, ids.shape[1]), 0)
    first = jnp.where(ids[0:1] == column, weights[0:1], 0.0)
    return first + jnp.where(ids[1:2] == column, weights[1:2], 0.0)


def silu_slope(preact):
    logistic = jax.nn.sigmoid(preact)
    return logistic * (1.0 + preact * (1.0 - logistic))


def mean_last(values):
    return jnp.mean(values, axis=-1, keepdims=True)


def fold(values):
    half = values.shape[1] // 2
    return jnp.concatenate([values[:, :half], values[:, half:]], axis=0)


def unfold(values):
    half = values.shape[0] // 2
    return jnp.concatenate([values[:half], values[half:]], axis=1)


def make_kernel(ny, nz, nx, width, nodes, edges, sends, coarse, cedges):
    half = width // CORES
    sizes = {"y": ny, "z": nz, "x": nx}
    plans = ((("z",), ("x", "y")), (("y",), ("x", "z")), (("x",), ("z",), ("y",)))

    def offsets(axes):
        places = [{}]
        for axis in axes:
            places = [{**place, axis: k} for place in places for k in range(sizes[axis])]
        return places

    def farthest_first(axes):
        places = offsets(axes)

        def hops(slot):
            return sum(min(k, sizes[axis] - k) for axis, k in places[slot].items())

        return sorted(range(1, len(places)), key=hops, reverse=True)
    table = nodes + nodes + 2 * sends
    reach, hops = 2, [1]
    while reach < max(ny, nz) // 2:
        hops.append(2)
        reach += 2
    hops.append(1)

    def vmem(*shape, kind=BF16):
        return pltpu.VMEM(shape, kind)

    def sems(*count):
        return pltpu.SemaphoreType.DMA(count)

    loaded = dict(
        node=vmem(nodes, width),
        edge=vmem(edges, width),
        cedge=vmem(cedges, width),
        ws=vmem(width, width),
        wt=vmem(width, width),
        wn=vmem(width, width),
        cot=vmem(nodes, width),
        halo=vmem(1, 2, sends, kind=I32),
        src=vmem(1, edges, kind=I32),
        dst=vmem(1, edges, kind=I32),
        csrc=vmem(1, cedges, kind=I32),
        cdst=vmem(1, cedges, kind=I32),
        ids=vmem(2, nodes, kind=I32),
        wts=vmem(2, nodes, kind=F32),
    )
    work = dict(
        oht=vmem(table, edges),
        oh=vmem(edges, table),
        proj=vmem(table, width),
        pre=vmem(edges, width, kind=F32),
        msg=vmem(edges, width),
        normed=vmem(nodes, width, kind=F32),
        fine_out=vmem(nodes, width, kind=F32),
        in_sem=sems(len(loaded)),
        hello=pltpu.SemaphoreType.REGULAR((len(hops),)),
    )

    def exchange(out, into, count):
        return dict(out=out, into=into, ss=sems(count), rs=sems(count))

    rows = vmem(2 * sends, width)
    halves = [exchange(rows, rows, 2) for _ in range(2)]
    sums = [exchange(vmem(coarse, width), vmem(nx - 1, coarse, width), nx - 1) for _ in range(2)]
    streams = []
    for i, plan in enumerate(plans):
        parts = 1
        first = vmem(parts, half, width // parts)
        levels = [exchange(first, first, parts)]
        size = half
        for axes in plan:
            count = len(offsets(axes))
            size = size // count
            if axes is plan[-1]:
                buffer = vmem(count - 1, size, width, kind=F32)
            elif axes is plan[0]:
                buffer = vmem(parts * (count - 1), size, width // parts)
            else:
                buffer = vmem(count - 1, 2 * size, width // 2)
            levels.append(exchange(buffer, buffer, buffer.shape[0]))
        streams.append(
            dict(
                perm=vmem(width, width),
                left=vmem(width, nodes + coarse + (2 * sends if i == 0 else 0)),
                keep=vmem(half, width, kind=F32),
                levels=levels,
            )
        )
    scratch = [loaded, work, halves, sums, streams]

    def kernel(*refs):
        count = len(loaded)
        given, outs = refs[:count], refs[count : count + 5]
        held, work, halves, sums, streams = refs[count + 5 :]
        v = SimpleNamespace(**held, **work)
        halves, sums = ([SimpleNamespace(**e) for e in group] for group in (halves, sums))
        streams = [SimpleNamespace(**stream) for stream in streams]
        for stream in streams:
            stream.levels = [SimpleNamespace(**level) for level in stream.levels]
        for stream, plan, row in zip(streams, plans, outs[2:]):
            stream.plan, stream.row = plan, row
            stream.parts = stream.levels[0].out.shape[0]
            step = width // stream.parts
            stream.columns = [slice(i * step, (i + 1) * step) for i in range(stream.parts)]
        source_stream, target_stream, node_stream = streams
        halo_rows, back_rows = halves
        cot_sum, val_sum = sums
        dom, x = lax.axis_index("dom"), lax.axis_index("grp")
        core = lax.rem(dom, CORES)
        z = lax.rem(lax.div(dom, CORES), nz)
        y = lax.div(dom, CORES * nz)
        ring = dict(
            x=[x] + [lax.rem(x + k, nx) for k in range(1, nx)],
            y=[y] + [lax.rem(y + k, ny) for k in range(1, ny)],
            z=[z] + [lax.rem(z + k, nz) for k in range(1, nz)],
        )

        loads = SimpleNamespace(
            **{
                name: pltpu.make_async_copy(ref, held[name], v.in_sem.at[i])
                for i, (name, ref) in enumerate(zip(loaded, given))
            }
        )

        def place(y, z, core, x):
            return ((y * nz + z) * CORES + core, x)

        def at(shift):
            return place(
                ring["y"][shift.get("y", 0)],
                ring["z"][shift.get("z", 0)],
                core,
                ring["x"][shift.get("x", 0)],
            )

        twin = place(y, z, 1 - core, x)
        total = ny * nz * CORES * nx
        here = dom * nx + x
        above, below = lax.rem(here + 1, total), lax.rem(here + total - 1, total)
        above, below = ((lax.div(n, nx), lax.rem(n, nx)) for n in (above, below))

        barrier = pltpu.get_barrier_semaphore()
        around = [at({"y": 1}), at({"y": ny - 1}), at({"z": 1}), at({"z": nz - 1})]
        partners = [above, below] + [at({"x": k}) for k in range(1, nx)] + around + [twin]
        for partner in partners:
            pl.semaphore_signal(barrier, inc=1, device_id=partner, device_id_type=MESH)

        for load in (
            loads.halo,
            loads.node,
            loads.src,
            loads.dst,
            loads.ids,
            loads.wts,
            loads.csrc,
            loads.cdst,
            loads.cot,
            loads.wt,
            loads.ws,
            loads.edge,
            loads.wn,
            loads.cedge,
        ):
            load.start()

        def tell(step):
            hop = hops[step]
            for shift in ({"y": hop}, {"y": ny - hop}, {"z": hop}, {"z": nz - hop}):
                pl.semaphore_signal(
                    v.hello.at[step], inc=1, device_id=at(shift), device_id_type=MESH
                )

        def hear(step):
            pl.semaphore_wait(v.hello.at[step], len(around))

        def remote(source, target, send_sem, recv_sem, device):
            return pltpu.make_async_remote_copy(
                src_ref=source,
                dst_ref=target,
                send_sem=send_sem,
                recv_sem=recv_sem,
                device_id=device,
                device_id_type=MESH,
            )

        started = []

        def settle():
            for copy in started:
                copy.wait_send()
            started.clear()

        def start(copies):
            for copy in copies:
                copy.start()
            started.extend(copies)
            return copies

        loads.halo.wait()
        lists = v.halo[0]
        side = [one_hot(lists[s : s + 1], nodes) for s in range(2)]
        loads.node.wait()
        node = v.node[...]
        for s in range(2):
            halo_rows.out[s * sends : (s + 1) * sends] = tn(side[s], node).astype(BF16)
        low, high = pl.ds(0, sends), pl.ds(sends, sends)
        pl.semaphore_wait(barrier, len(partners))

        def to_neighbours(e):
            return start(
                [
                    remote(e.out.at[low], e.into.at[high], e.ss.at[0], e.rs.at[0], below),
                    remote(e.out.at[high], e.into.at[low], e.ss.at[1], e.rs.at[1], above),
                ]
            )

        def to_peer(e, source, axes, slot, base=-1):
            i = base + slot
            copy = remote(
                source, e.into.at[i], e.ss.at[i], e.rs.at[i], at(offsets(axes)[slot])
            )
            return start([copy])[0]

        def to_group(e):
            return [to_peer(e, e.out, ("x",), slot) for slot in farthest_first(("x",))]

        def group_sum(e, copies):
            for copy in copies:
                copy.wait_recv()
            running = e.out[...].astype(F32)
            for k in range(nx - 1):
                running = running + e.into[k].astype(F32)
            return running

        halo = to_neighbours(halo_rows)
        tell(0)
        loads.ids.wait()
        loads.wts.wait()
        restrict = restriction(v.ids[...], v.wts[...], coarse).astype(BF16)
        loads.cot.wait()
        cot_sum.out[...] = nn(restrict, v.cot[...]).astype(BF16)
        cot_copies = to_group(cot_sum)

        loads.src.wait()
        loads.dst.wait()
        v.oht[0:nodes] = one_hot(v.dst[...], nodes)
        v.oht[nodes:] = one_hot(v.src[...], table - nodes)
        eye = hot(iota((edges, edges), 0) == iota((edges, edges), 1))
        v.oh[...] = nt(eye, v.oht[...]).astype(BF16)
        loads.wt.wait()
        v.proj[0:nodes] = nn(node, v.wt[...]).astype(BF16)
        loads.ws.wait()
        v.proj[nodes : 2 * nodes] = nn(node, v.ws[...]).astype(BF16)
        loads.edge.wait()
        chunk = edges // 4
        local = 2 * nodes
        for e in range(0, edges, chunk):
            rows = slice(e, e + chunk)
            v.pre[rows] = v.edge[rows].astype(F32) + nn(
                v.oh[rows, 0:local], v.proj[0:local]
            )
        for copy in halo:
            copy.wait_recv()
        hear(0)
        tell(1)
        v.proj[local:] = nn(halo_rows.into[...], v.ws[...]).astype(BF16)
        for e in range(0, edges, chunk):
            rows = slice(e, e + chunk)
            preact = v.pre[rows] + nn(v.oh[rows, local:], v.proj[local:])
            v.pre[rows] = preact
            v.msg[rows] = jax.nn.silu(preact).astype(BF16)
        summed = nn(v.oht[0:nodes], v.msg[...])
        inverse = lax.rsqrt(mean_last(summed * summed) + EPSILON)
        normed = summed * inverse
        v.normed[...] = normed
        normed_half = normed.astype(BF16)
        loads.wn.wait()
        fine_out = node.astype(F32) + nn(normed_half, v.wn[...])
        v.fine_out[...] = fine_out
        val_sum.out[...] = nn(restrict, fine_out.astype(BF16)).astype(BF16)
        val_copies = to_group(val_sum)

        for stream in streams:
            order = [axis for axes in stream.plan for axis in axes]
            rest = iota((width, width), 0)
            digits = {}
            for axis in reversed(order):
                digits[axis] = rest % sizes[axis]
                rest = rest // sizes[axis]
            owner_core = jnp.where(rest == 0, 1 - core, core)
            row = ((y + digits["y"]) % ny) * nz + (z + digits["z"]) % nz
            row = (row * CORES + owner_core) * nx + (x + digits["x"]) % nx
            stream.perm[...] = hot(row == iota((width, width), 1))
        source_stream.left[:, 0:nodes] = nt(source_stream.perm[...], node).astype(BF16)
        source_stream.left[:, nodes : nodes + 2 * sends] = nt(
            source_stream.perm[...], halo_rows.into[...]
        ).astype(BF16)
        target_stream.left[:, 0:nodes] = nt(target_stream.perm[...], node).astype(BF16)
        node_stream.left[:, 0:nodes] = nt(node_stream.perm[...], normed_half).astype(BF16)
        for stream in streams:
            stream.left[:, -coarse:] = jnp.zeros((width, coarse), BF16)
        for e in range(0, edges, chunk):
            rows = slice(e, e + chunk)
            v.pre[rows] = silu_slope(v.pre[rows])
        loads.csrc.wait()
        loads.cdst.wait()
        coarse_hot_t = jnp.concatenate(
            [one_hot(v.cdst[...], coarse), one_hot(v.csrc[...], coarse)], axis=0
        )
        eye = hot(iota((cedges, cedges), 0) == iota((cedges, cedges), 1))
        coarse_hot = nt(eye, coarse_hot_t).astype(BF16)
        eye = hot(iota((nodes, nodes), 0) == iota((nodes, nodes), 1))
        prolong = nt(eye, restrict).astype(BF16)
        grad_coarse = group_sum(cot_sum, cot_copies)
        grad_coarse_half = grad_coarse.astype(BF16)
        coarse_normed_grad = nt(grad_coarse_half, v.wn[...])
        loads.cedge.wait()
        coarse_edge = v.cedge[...].astype(F32)

        for step in range(1, len(hops) - 1):
            hear(step)
            tell(step + 1)
        coarse_half = group_sum(val_sum, val_copies).astype(BF16)
        coarse_proj = jnp.concatenate(
            [nn(coarse_half, v.wt[...]), nn(coarse_half, v.ws[...])], axis=0
        ).astype(BF16)
        quarter = width // nx
        rows = pl.ds(pl.multiple_of(x * quarter, quarter), quarter)
        preact = coarse_edge + nn(coarse_hot, coarse_proj)
        target_stream.left[rows, nodes:] = nt(target_stream.perm[rows], coarse_half).astype(BF16)
        source_stream.left[rows, nodes + 2 * sends :] = nt(
            source_stream.perm[rows], coarse_half
        ).astype(BF16)
        message = jax.nn.silu(preact).astype(BF16)
        summed = nn(coarse_hot_t[0:coarse], message)
        coarse_inverse = lax.rsqrt(mean_last(summed * summed) + EPSILON)
        coarse_normed = summed * coarse_inverse
        coarse_normed_half = coarse_normed.astype(BF16)
        for begin in range(0, width, half):
            rows = slice(begin, begin + half // nx)
            node_stream.left[rows, nodes:] = nt(node_stream.perm[rows], coarse_normed_half).astype(
                BF16
            )
        grad_summed = coarse_inverse * (
            coarse_normed_grad - coarse_normed * mean_last(coarse_normed_grad * coarse_normed)
        )
        grad_preact = (
            nn(coarse_hot[:, 0:coarse], grad_summed.astype(BF16)) * silu_slope(preact)
        ).astype(BF16)
        coarse_grad = nn(coarse_hot_t, grad_preact).astype(BF16)
        grad_coarse_in = (
            grad_coarse
            + nt(coarse_grad[coarse:], v.ws[...])
            + nt(coarse_grad[0:coarse], v.wt[...])
        )
        grad_fine = v.cot[...].astype(F32) + nn(prolong, grad_coarse_in.astype(BF16))
        grad_half = grad_fine.astype(BF16)

        def stage0(stream, right, part=0):
            e = stream.levels[0]
            e.out[part] = nn(stream.left[0:half], right).astype(BF16)
            copy = remote(e.out.at[part], e.into.at[part], e.ss.at[part], e.rs.at[part], twin)
            return start([copy])[0]

        def stage0_own(stream, right, part=0):
            stream.keep[:, stream.columns[part]] = nn(stream.left[half:], right)

        def stage1(group, copies, part=0):
            for copy in copies:
                copy.wait_recv()
            sent = [[] for _ in group]
            for slots in zip(*(farthest_first(stream.plan[0]) for stream in group)):
                for stream, slot, into in zip(group, slots, sent):
                    e, axes = stream.levels[1], stream.plan[0]
                    count = len(offsets(axes))
                    size = half // count
                    rows = slice(slot * size, (slot + 1) * size)
                    i = part * (count - 1) + slot - 1
                    e.out[i] = (
                        stream.keep[rows, stream.columns[part]]
                        + stream.levels[0].into[part, rows].astype(F32)
                    ).astype(BF16)
                    into.append(to_peer(e, e.out.at[i], axes, slot, part * (count - 1) - 1))
            for stream in group:
                rows = slice(0, half // len(offsets(stream.plan[0])))
                columns = stream.columns[part]
                stream.keep[rows, columns] = stream.keep[rows, columns] + stream.levels[0].into[
                    part, rows
                ].astype(F32)
            return sent

        def received1(stream, copies):
            slots = farthest_first(stream.plan[0])
            size = half // (len(slots) + 1)
            halves = []
            for part, columns in enumerate(stream.columns):
                running = stream.keep[0:size, columns]
                for slot, copy in zip(reversed(slots), reversed(copies[part])):
                    copy.wait_recv()
                    i = part * len(slots) + slot - 1
                    running = running + stream.levels[1].into[i].astype(F32)
                halves.append(running)
            return jnp.concatenate(halves, axis=1)

        def stage2(stream, copies):
            axes = stream.plan[1]
            running = received1(stream, [copies])
            size = running.shape[0] // len(offsets(axes))
            e, sent = stream.levels[2], []
            for slot in farthest_first(axes):
                part = fold(running[slot * size : (slot + 1) * size])
                e.out[slot - 1] = part.astype(BF16)
                sent.append(to_peer(e, e.out.at[slot - 1], axes, slot))
            return sent, running[0:size]

        def received2(stream, state):
            copies, running = state
            for copy in reversed(copies):
                copy.wait_recv()
            for k in range(len(copies)):
                running = running + unfold(stream.levels[2].into[k].astype(F32))
            return running

        def last(stream, running, slots):
            e, axes, sent = stream.levels[-1], stream.plan[-1], []
            for slot in slots:
                e.out[slot - 1] = running[slot : slot + 1]
                sent.append(to_peer(e, e.out.at[slot - 1], axes, slot))
            return sent

        def halved(slots):
            middle = len(slots) // 2
            return slots[:middle], slots[middle:]

        def finish(stream, copies, running):
            for copy in reversed(copies):
                copy.wait_recv()
            stream.row[...] = running[0:1] + jnp.sum(stream.levels[-1].into[...], axis=0)

        right = jnp.concatenate([grad_half, grad_coarse_half], axis=0)
        node_state = stage0(node_stream, right)

        grad_normed = nt(grad_half, v.wn[...])
        normed = v.normed[...]
        grad_summed = inverse * (grad_normed - normed * mean_last(grad_normed * normed))
        grad_summed = grad_summed.astype(BF16)
        edge_streams = (target_stream, source_stream)
        rights, twins = [], []
        for part, columns in enumerate(target_stream.columns):
            for e in range(0, edges, chunk):
                rows = slice(e, e + chunk)
                part_grad = nn(v.oh[rows, 0:nodes], grad_summed[:, columns])
                v.msg[rows, columns] = (part_grad * v.pre[rows, columns]).astype(BF16)
            scattered = nn(v.oht[...], v.msg[:, columns]).astype(BF16)
            rights.append(
                [
                    jnp.concatenate([scattered[0:nodes], coarse_grad[0:coarse, columns]], axis=0),
                    jnp.concatenate([scattered[nodes:], coarse_grad[coarse:, columns]], axis=0),
                ]
            )
            twins.append(
                [stage0(stream, r, part) for stream, r in zip(edge_streams, rights[-1])]
            )
        stage0_own(node_stream, right)
        node_state = stage1([node_stream], [node_state])[0]
        target_state, source_state = [], []
        for part in range(len(twins)):
            for stream, r in zip(edge_streams, rights[part]):
                stage0_own(stream, r, part)
        for part in range(len(twins)):
            to_target, to_source = stage1(edge_streams, twins[part], part)
            target_state.append(to_target)
            source_state.append(to_source)
        grad_dst, grad_src = (
            jnp.concatenate([part[i][:count] for part in rights], axis=1)
            for i, count in ((0, nodes), (1, nodes + 2 * sends))
        )
        back_rows.out[...] = nt(grad_src[nodes:], v.ws[...]).astype(BF16)
        back = to_neighbours(back_rows)
        grad_latent = grad_fine + nt(grad_src[0:nodes], v.ws[...]) + nt(grad_dst, v.wt[...])
        coarse_out = coarse_half.astype(F32) + nn(coarse_normed_half, v.wn[...])
        updated = v.fine_out[...] + nn(prolong, coarse_out.astype(BF16))
        outs[0][...] = updated.astype(BF16)
        node_state = stage2(node_stream, node_state)
        for copy in back:
            copy.wait_recv()
        for s in range(2):
            grad_latent = grad_latent + nn(side[s], back_rows.into[s * sends : (s + 1) * sends])
        outs[1][...] = grad_latent.astype(BF16)
        target_far, target_near = halved(farthest_first(target_stream.plan[-1]))
        source_far, source_near = halved(farthest_first(source_stream.plan[-1]))
        hear(len(hops) - 1)
        target_sum = received1(target_stream, target_state)
        target_state = last(target_stream, target_sum, target_far)
        source_sum = received1(source_stream, source_state)
        source_state = last(source_stream, source_sum, source_far)
        node_sum = received2(node_stream, node_state)
        node_state = last(node_stream, node_sum, farthest_first(node_stream.plan[-1]))
        target_state += last(target_stream, target_sum, target_near)
        source_state += last(source_stream, source_sum, source_near)
        settle()
        finish(node_stream, node_state, node_sum)
        finish(target_stream, target_state, target_sum)
        finish(source_stream, source_state, source_sum)

    return kernel, scratch


def write_out(*refs):
    count = len(refs) // 2
    sems = refs[-1]
    copies = [pltpu.make_async_copy(refs[i], refs[count + i], sems.at[i]) for i in range(count)]
    for copy in copies:
        copy.start()
    for copy in copies:
        copy.wait()


def solution(mesh):
    nx = mesh.shape["grp"]
    chips = mesh.shape["dom"] // CORES
    ny = 1
    while ny * ny < chips:
        ny += 1
    nz = chips // ny

    def step(node, edge, cedge, ws, wt, wn, cot, halo, src, dst, csrc, cdst, ids, weights):
        nodes, width = node.shape
        kernel, scratch = make_kernel(
            ny,
            nz,
            nx,
            width,
            nodes,
            edge.shape[0],
            halo.shape[2],
            COARSE_DEV * nx,
            cedge.shape[0],
        )
        row = jax.ShapeDtypeStruct((1, width), F32)
        rows = jax.ShapeDtypeStruct((nodes, width), BF16)
        shapes = (rows, rows, row, row, row)
        lists = [given.reshape(1, -1) for given in (src, dst, csrc, cdst)]
        arguments = (node, edge, cedge, ws, wt, wn, cot, halo, *lists, ids, weights)
        held = pl.pallas_call(
            kernel,
            out_shape=tuple(pltpu.VMEM(shape.shape, shape.dtype) for shape in shapes),
            in_specs=[pl.BlockSpec(memory_space=pltpu.HBM)] * 14,
            out_specs=[pl.BlockSpec(memory_space=pltpu.VMEM)] * 5,
            scratch_shapes=scratch,
            compiler_params=pltpu.CompilerParams(
                collective_id=0, has_side_effects=True, vmem_limit_bytes=VMEM_BYTES
            ),
        )(*(pltpu.with_memory_space_constraint(given, pltpu.HBM) for given in arguments))
        updated, latent, gs, gt, gn = pl.pallas_call(
            write_out,
            out_shape=shapes,
            in_specs=[pl.BlockSpec(memory_space=pltpu.VMEM)] * 5,
            out_specs=[pl.BlockSpec(memory_space=pltpu.HBM)] * 5,
            scratch_shapes=[pltpu.SemaphoreType.DMA((5,))],
            compiler_params=pltpu.CompilerParams(vmem_limit_bytes=VMEM_BYTES),
        )(*held)
        return updated, latent, gs.reshape(-1), gt.reshape(-1), gn.reshape(-1)

    fine = P(("dom", "grp"), None)
    flat = P(("dom", "grp"))
    return jax.shard_map(
        step,
        mesh=mesh,
        in_specs=(
            fine,
            fine,
            P("dom", None),
            P(),
            P(),
            P(),
            fine,
            P(("dom", "grp"), None, None),
            flat,
            flat,
            P("dom"),
            P("dom"),
            P(None, ("dom", "grp")),
            P(None, ("dom", "grp")),
        ),
        out_specs=(fine, fine, flat, flat, flat),
        check_vma=False,
    )
```
